32 devices in a mesh: rows: 8 (over z, x), rep: 4 (over y, core).
Axes of the slice: x: 2, y: 2, z: 4, core: 2. Of those that a mesh axis runs over, the one named last changes fastest.
Arguments:
- feats: bfloat16 [4, 2048, 512], P('rep', 'rows'), may hold values from -24 to 24
- grad_out: bfloat16 [4, 2048, 512], P('rep', 'rows'), may hold values from -6 to 6
- qkv_weight: bfloat16 [512, 1536], P('rows'), may hold values from -0.25 to 0.25
- proj_weight: bfloat16 [512, 512], P('rows'), may hold values from -0.25 to 0.25
- to_hilbert: int32 [4, 64], P('rep', 'rows'), may hold values from 0 to 63, as said below
- to_zorder: int32 [4, 64], P('rep', 'rows'), may hold values from 0 to 63, as said below
Outputs:
- grad_feats: bfloat16 [4, 2048, 512], P('rep', 'rows')
- qkv_grad: float32 [512, 1536], P('rows')
- proj_grad: float32 [512, 512], P('rows')
The draws below stay inside these ranges and needn't reach their ends.
Inputs may be any that keep to these rules, and one draw needn't show every extreme that they name: to_hilbert[s] is a permutation of the blocks of scene s and to_zorder[s] its inverse; of the 8 Z-order blocks of one device, at most 2 have Hilbert positions on any one device, and exactly 2 for some pair of devices in every scene. `to_zorder`: the inverse of to_hilbert in every scene.
All inputs are finite; a program needn't handle non-finite values.
Results may differ from the reference program's by a relative error of at most 0.015.
The reference program's roundings to bfloat16 on the way (of `qkv`, `grad_hil`, `grad_attn`, `probs_b`, `attn`, `dscore`, `grad_qkv` and `grad_hfeat`) count: a program that leaves them out, or rounds other values in their place, can miss the bound.
Values may be sent and summed in bfloat16 or wider, within the bound.
A program may use at most 64 MiB of HBM per device.

```python
import jax
import jax.numpy as jnp
from jax import lax

C = 512
HEADS = 8
HD = 64
PATCH = 512
BLK = 32
POINTS = 2048
BLOCKS = 64
SCENES = 4
N_ROWS = 8


def block_orders(key):
    peers = N_ROWS

    def one_scene(scene_key):
        key_shift, key_rot, key_slot = jax.random.split(scene_key, 3)
        chosen = jax.random.permutation(key_shift, peers)
        quarter = peers // 4
        half = peers // 2
        shifts = jnp.concatenate([chosen[:quarter], chosen[:quarter], chosen[quarter:quarter + half]])
        rotation = jax.random.randint(key_rot, (peers,), 0, peers)
        source = jnp.arange(peers, dtype=jnp.int32)[:, None]
        column = jnp.arange(peers, dtype=jnp.int32)[None, :]
        target = (source + shifts[(column + rotation[:, None]) % peers]) % peers
        flat = target.reshape(-1).astype(jnp.int32)
        order = jnp.argsort(flat, stable=True)
        position = jnp.zeros(peers * peers, jnp.int32).at[order].set(jnp.arange(peers * peers, dtype=jnp.int32))
        rank_in = position - flat * peers
        slot_keys = jax.random.split(key_slot, peers)
        shuffles = jax.vmap(lambda inner: jax.random.permutation(inner, peers))(slot_keys).astype(jnp.int32)
        forward_list = flat * peers + shuffles[flat, rank_in]
        inverse_list = jnp.zeros(peers * peers, jnp.int32).at[forward_list].set(jnp.arange(peers * peers, dtype=jnp.int32))
        return (forward_list, inverse_list)
    scene_keys = jax.random.split(key, SCENES)
    return jax.vmap(one_scene)(scene_keys)


def draw_to_hilbert(key, part):
    return block_orders(jax.random.fold_in(key, 7))[0]


def draw_to_zorder(key, part):
    return block_orders(jax.random.fold_in(key, 7))[1]


def draw_feats(key, part):
    key_main = jax.random.fold_in(key, 0)
    values = jnp.clip(jax.random.normal(key_main, (SCENES, POINTS, C), jnp.float32), -4.0, 4.0)
    return values.astype(jnp.bfloat16)


def block_scale(rng, extent, cuts, smallest, top_value):
    def one(dim, shards_of):
        steps = jax.random.uniform(jax.random.fold_in(jax.random.fold_in(rng, 6), dim), (shards_of,), jnp.float32, smallest / len(cuts), top_value / len(cuts))
        return jnp.repeat(jnp.exp(steps), extent[dim] // shards_of).reshape((-1,) + (1,) * (len(extent) - dim - 1))

    gain = one(*cuts[0])
    for cut in cuts[1:]:
        gain = gain * one(*cut)
    return gain


def noise(stream_key, dims, width, most, shards=(), kind=jnp.bfloat16):
    entries = width * jax.random.normal(stream_key, dims, jnp.float32)
    if shards:
        entries = entries * block_scale(stream_key, dims, shards, -0.22, 0.18)
    return jnp.clip(entries, -most, most).astype(kind)


def setup_inputs(seed: int = 0) -> dict:
    splits = jax.random.split(jax.random.key(seed), 7)
    feats = draw_feats(jax.random.fold_in(splits[6], 71), 0)
    grad_out = noise(splits[1], (SCENES, POINTS, C), 1.0, 6.0, ((0, 4), (1, 8)))
    qkv_weight = noise(splits[2], (C, 3 * C), C ** -0.5, 0.25, ((0, 8),))
    proj_weight = noise(splits[3], (C, C), C ** -0.5, 0.25, ((0, 8),))
    to_hilbert = draw_to_hilbert(jax.random.fold_in(splits[6], 71), 0)
    to_zorder = draw_to_zorder(jax.random.fold_in(splits[6], 71), 0)
    return {"feats": feats, "grad_out": grad_out, "qkv_weight": qkv_weight, "proj_weight": proj_weight, "to_hilbert": to_hilbert, "to_zorder": to_zorder}


def patch_backward(qkv_patch, grad_patch):
    scale = HD ** -0.5
    qf = qkv_patch[:, :C].astype(jnp.float32).reshape(PATCH, HEADS, HD)
    kf = qkv_patch[:, C:2 * C].astype(jnp.float32).reshape(PATCH, HEADS, HD)
    vf = qkv_patch[:, 2 * C:].astype(jnp.float32).reshape(PATCH, HEADS, HD)
    gf = grad_patch.astype(jnp.float32).reshape(PATCH, HEADS, HD)
    score = jnp.einsum('qhd,khd->hqk', qf, kf) * scale
    row_max = jnp.max(score, axis=-1, keepdims=True)
    raised = jnp.exp(score - row_max)
    row_sum = jnp.sum(raised, axis=-1, keepdims=True)
    probs = raised / row_sum
    probs_b = probs.astype(jnp.bfloat16).astype(jnp.float32)
    attn = jnp.einsum('hqk,khd->qhd', probs_b, vf).astype(jnp.bfloat16).reshape(PATCH, C)
    dprob = jnp.einsum('qhd,khd->hqk', gf, vf)
    delta = jnp.sum(probs * dprob, axis=-1, keepdims=True)
    dscore = (probs * (dprob - delta) * scale).astype(jnp.bfloat16).astype(jnp.float32)
    grad_q = jnp.einsum('hqk,khd->qhd', dscore, kf).reshape(PATCH, C)
    grad_k = jnp.einsum('hqk,qhd->khd', dscore, qf).reshape(PATCH, C)
    grad_v = jnp.einsum('hqk,qhd->khd', probs_b, gf).reshape(PATCH, C)
    grad_qkv = jnp.concatenate([grad_q, grad_k, grad_v], axis=1).astype(jnp.bfloat16)
    return attn, grad_qkv


def scene_backward(feat, grad_z, forward_list, inverse_list, qkv_weight, proj_weight):
    grad_hil = grad_z.reshape(BLOCKS, BLK * C)[inverse_list].reshape(POINTS, C)
    qkv = jnp.dot(feat, qkv_weight, preferred_element_type=jnp.float32).astype(jnp.bfloat16)
    grad_attn = jnp.dot(grad_hil, proj_weight.T, preferred_element_type=jnp.float32).astype(jnp.bfloat16)
    patches = POINTS // PATCH
    attn, grad_qkv = lax.map(lambda pair: patch_backward(pair[0], pair[1]),
                             (qkv.reshape(patches, PATCH, 3 * C), grad_attn.reshape(patches, PATCH, C)))
    attn = attn.reshape(POINTS, C)
    grad_qkv = grad_qkv.reshape(POINTS, 3 * C)
    grad_hfeat = jnp.dot(grad_qkv, qkv_weight.T, preferred_element_type=jnp.float32).astype(jnp.bfloat16)
    grad_feat = grad_hfeat.reshape(BLOCKS, BLK * C)[forward_list].reshape(POINTS, C)
    qkv_term = jnp.dot(feat.T, grad_qkv, preferred_element_type=jnp.float32)
    proj_term = jnp.dot(attn.T, grad_hil, preferred_element_type=jnp.float32)
    return grad_feat, qkv_term, proj_term


def reference(feats, grad_out, qkv_weight, proj_weight, to_hilbert, to_zorder):
    grads = []
    qkv_grad = jnp.zeros((C, 3 * C), jnp.float32)
    proj_grad = jnp.zeros((C, C), jnp.float32)
    for scene in range(SCENES):
        grad_feat, qkv_term, proj_term = scene_backward(feats[scene], grad_out[scene], to_hilbert[scene],
                                                        to_zorder[scene], qkv_weight, proj_weight)
        grads.append(grad_feat)
        qkv_grad = qkv_grad + qkv_term
        proj_grad = proj_grad + proj_term
    return jnp.stack(grads, axis=0), qkv_grad, proj_grad
```

```python
import jax
import jax.numpy as jnp
from jax import lax
from jax.experimental import pallas as pl
from jax.experimental.pallas import tpu as pltpu
from jax.sharding import PartitionSpec as P

HEADS = 8
CAP = 2


def from_partner(block, axis, apart):
    count = lax.axis_size(axis)
    route = []
    for low in range(count):
        high = low | 1 << apart
        if high != low and high < count:
            route += [(low, high), (high, low)]
    return lax.ppermute(block, axis, route)


def move_blocks(outgoing):
    return lax.all_to_all(outgoing, "rows", split_axis=0, concat_axis=0, tiled=True)


def rank_within(order_keys, owners):
    same_owner = owners[None, :] == owners[:, None]
    earlier = order_keys[None, :] < order_keys[:, None]
    return jnp.sum(jnp.logical_and(same_owner, earlier).astype(jnp.int32), axis=1)


def contract_rows(left, right):
    return lax.dot_general(
        left, right, (((0,), (0,)), ((), ())), preferred_element_type=jnp.float32
    )


def contract_cols(left, right):
    return lax.dot_general(
        left, right, (((1,), (1,)), ((), ())), preferred_element_type=jnp.float32
    )


def per_device_general(feats, grad_out, qkv_weight, proj_weight, to_hilbert, to_zorder):
    peer_count = lax.axis_size("rows")
    feature = feats[0]
    rows_dev, channels = feature.shape
    head_size = channels // HEADS
    scale = head_size ** (-0.5)
    blocks_dev = to_hilbert.shape[1]
    slot_count = peer_count * CAP
    w_qkv, w_proj = (
        lax.all_gather(qkv_weight, "rows", axis=0, tiled=True),
        lax.all_gather(proj_weight, "rows", axis=0, tiled=True),
    )
    forward_list = to_hilbert[0]
    inverse_list = to_zorder[0]
    local_ids = jnp.arange(blocks_dev, dtype=jnp.int32)
    slot_ids = jnp.arange(slot_count, dtype=jnp.int32)
    target_dev = forward_list // blocks_dev
    send_slot = target_dev * CAP + rank_within(local_ids, target_dev)
    send_table = (send_slot[None, :] == slot_ids[:, None]).astype(jnp.bfloat16)
    source_dev = inverse_list // blocks_dev
    recv_slot = source_dev * CAP + rank_within(inverse_list, source_dev)
    recv_table = (recv_slot[:, None] == slot_ids[None, :]).astype(jnp.bfloat16)
    zblocks = grad_out[0].reshape(blocks_dev, -1)
    outgoing = jnp.dot(send_table, zblocks, preferred_element_type=jnp.float32).astype(jnp.bfloat16)
    arrived = move_blocks(outgoing.reshape(peer_count, CAP, -1)).reshape(slot_count, -1)
    grad_hil = jnp.dot(recv_table, arrived, preferred_element_type=jnp.float32).astype(jnp.bfloat16)
    grad_hil = grad_hil.reshape(rows_dev, channels)
    qkv = jnp.dot(feature, w_qkv, preferred_element_type=jnp.float32).astype(jnp.bfloat16)
    query = qkv[:, :channels]
    keyval = qkv[:, channels:]
    grad_attn = contract_cols(grad_hil, w_proj).astype(jnp.bfloat16)
    other_kv = from_partner(keyval, "rows", 0)
    keys_all = jnp.concatenate([keyval[:, :channels], other_kv[:, :channels]], axis=0)
    values_all = jnp.concatenate([keyval[:, channels:], other_kv[:, channels:]], axis=0)
    attn_parts, dq_parts, dk_parts, dv_parts = ([], [], [], [])
    for head_index in range(HEADS):
        lo_col = head_index * head_size
        q_head = query[:, lo_col : lo_col + head_size]
        k_head = keys_all[:, lo_col : lo_col + head_size]
        v_head = values_all[:, lo_col : lo_col + head_size]
        g_head = grad_attn[:, lo_col : lo_col + head_size]
        score = contract_cols(q_head, k_head) * scale
        row_max = jnp.max(score, axis=1, keepdims=True)
        raised = jnp.exp(score - row_max)
        row_sum = jnp.sum(raised, axis=1, keepdims=True)
        probs = raised / row_sum
        probs_b = probs.astype(jnp.bfloat16)
        attn_parts.append(
            jnp.dot(probs_b, v_head, preferred_element_type=jnp.float32).astype(jnp.bfloat16)
        )
        dprob = contract_cols(g_head, v_head)
        delta = jnp.sum(probs * dprob, axis=1, keepdims=True)
        dscore = (probs * (dprob - delta) * scale).astype(jnp.bfloat16)
        dq_parts.append(jnp.dot(dscore, k_head, preferred_element_type=jnp.float32))
        dk_parts.append(contract_rows(dscore, q_head))
        dv_parts.append(contract_rows(probs_b, g_head))
    grad_q = jnp.concatenate(dq_parts, axis=1)
    grad_k = jnp.concatenate(dk_parts, axis=1)
    grad_v = jnp.concatenate(dv_parts, axis=1)
    other_k, other_v = (
        from_partner(grad_k[rows_dev:].astype(jnp.bfloat16), "rows", 0).astype(jnp.float32),
        from_partner(grad_v[rows_dev:].astype(jnp.bfloat16), "rows", 0).astype(jnp.float32),
    )
    grad_k = grad_k[:rows_dev] + other_k
    grad_v = grad_v[:rows_dev] + other_v
    grad_qkv = jnp.concatenate([grad_q, grad_k, grad_v], axis=1).astype(jnp.bfloat16)
    attn = jnp.concatenate(attn_parts, axis=1)
    grad_hfeat = contract_cols(grad_qkv, w_qkv).astype(jnp.bfloat16)
    hblocks = grad_hfeat.reshape(blocks_dev, -1)
    going_back = contract_rows(recv_table, hblocks).astype(jnp.bfloat16)
    returned = move_blocks(going_back.reshape(peer_count, CAP, -1)).reshape(slot_count, -1)
    grad_z = contract_rows(send_table, returned).astype(jnp.bfloat16).reshape(rows_dev, channels)
    share = channels // peer_count
    term = jnp.concatenate(
        [contract_rows(feature, grad_qkv), contract_rows(attn, grad_hil)], axis=1
    )
    total = lax.psum(term, ("rows", "rep"))
    owned = lax.dynamic_slice_in_dim(total, lax.axis_index("rows") * share, share, 0)
    return (grad_z[None], owned[:, : 3 * channels], owned[:, 3 * channels :])


MESH = pl.DeviceIdType.MESH
PAIR = 128
STRIP = 16
F32 = jnp.float32
BF16 = jnp.bfloat16


def dot(left, right):
    return jnp.dot(left, right, preferred_element_type=F32)


def fused_kernel(peers, slot_rows, feats_ref, grad_ref, wq_ref, wp_ref, srow_ref, rrow_ref,
                 gf_ref, qg_ref, pg_ref,
                 wf, wz_s, wz_r, wx_s, wx_r, wy_s, wy_r, wc_s, wc_r,
                 out_buf, arr_buf, sl_s, sl_r, back_buf, ret_buf, bk_s, bk_r,
                 fa, ft, ff_s, ff_r, q_v, k_v, v_v, g_v, h_v, at_v, dq_v, dk_v, dv_v,
                 dks, dkr, dk_s, dk_r, red_s, red_r, *reds):
    rows, channels = feats_ref.shape
    pairs = channels // PAIR
    r = lax.axis_index("rows")
    p = lax.axis_index("rep")
    x, z = lax.rem(r, 2), lax.div(r, 2)
    c, y = lax.rem(p, 2), lax.div(p, 2)
    across_x = (r + 1 - 2 * x, p)
    across_c = (r, p + 1 - 2 * c)
    across_y = (r, p + 2 - 4 * y)
    zs = peers // 2
    sends = []

    def send(src, dst, send_sem, recv_sem, device):
        copy = pltpu.make_async_remote_copy(
            src_ref=src, dst_ref=dst, send_sem=send_sem, recv_sem=recv_sem,
            device_id=device, device_id_type=MESH)
        copy.start()
        sends.append(copy)
        return copy

    barrier = pltpu.get_barrier_semaphore()
    for k in range(1, peers):
        pl.semaphore_signal(barrier, inc=1, device_id=(lax.rem(r + k, peers), p), device_id_type=MESH)
    for k in range(1, 4):
        pl.semaphore_signal(barrier, inc=1, device_id=(r, lax.rem(p + k, 4)), device_id_type=MESH)

    wide = wq_ref.shape[1]
    for strip in range(4):
        wf[r, strip, :, 0:wide] = wq_ref[strip * STRIP : (strip + 1) * STRIP, :]
        wf[r, strip, :, wide:] = wp_ref[strip * STRIP : (strip + 1) * STRIP, :]
    slot_ids = lax.broadcasted_iota(jnp.int32, (slot_rows, rows), 0)
    pack = jnp.where(slot_ids == srow_ref[...], 1.0, 0.0).astype(BF16)
    per_peer = slot_rows // peers
    out_buf[...] = dot(pack, grad_ref[...]).astype(BF16).reshape(peers, per_peer, channels)
    arr_buf[r] = out_buf[r]
    fa[0] = feats_ref[...]
    pl.semaphore_wait(barrier, peers - 1 + 3)

    z_copies = []
    for k in range(1, zs):
        to = (lax.rem(z + k, zs) * 2 + x, p)
        z_copies.append(send(wf.at[r, p], wf.at[r, p], wz_s.at[k - 1], wz_r.at[k - 1], to))
    x_copies = [send(wf.at[r, p], wf.at[r, p], wx_s.at[0], wx_r.at[0], across_x)]
    f_copy = send(feats_ref, fa.at[1], ff_s, ff_r, across_x)
    slot_copies = []
    for k in range(1, peers):
        d = lax.rem(r + k, peers)
        slot_copies.append(send(out_buf.at[d], arr_buf.at[r], sl_s.at[k - 1], sl_r.at[k - 1], (d, p)))
    y_copies, c_copies = [], []

    def to_y(row):
        i = len(y_copies)
        y_copies.append((send(wf.at[row, p], wf.at[row, p], wy_s.at[i], wy_r.at[i], across_y), row))

    def to_c(row, strip):
        i = len(c_copies)
        c_copies.append(send(wf.at[row, strip], wf.at[row, strip], wc_s.at[i], wc_r.at[i], across_c))

    for k in range(1, zs):
        z_copies[k - 1].wait_recv()
        row = lax.rem(z + zs - k, zs) * 2 + x
        x_copies.append(send(wf.at[row, p], wf.at[row, p], wx_s.at[k], wx_r.at[k], across_x))
        to_y(row)
        to_c(row, p)
    for k in range(zs):
        x_copies[k].wait_recv()
        row = lax.rem(z + zs - k, zs) * 2 + 1 - x
        to_y(row)
        to_c(row, p)
    f_copy.wait_recv()
    for i in range(2):
        ft[:, i * rows : (i + 1) * rows] = fa[i].astype(F32).T.astype(BF16)
    for copy, row in y_copies:
        copy.wait_recv()
        to_c(row, p + 2 - 4 * y)
    for copy in slot_copies:
        copy.wait_recv()
    place = jnp.where(slot_ids == rrow_ref[...], 1.0, 0.0).astype(BF16)
    h_v[...] = contract_rows(place, arr_buf[...].reshape(slot_rows, channels)).astype(BF16)
    for copy in c_copies:
        copy.wait_recv()

    def weight(lo, hi):
        return wf[:, :, :, lo:hi].reshape(4 * STRIP * peers, hi - lo)

    q_v[...] = dot(feats_ref[...], weight(0, channels)).astype(BF16)
    for i in range(2):
        part = slice(i * rows, (i + 1) * rows)
        k_v[part, :] = dot(fa[i], weight(channels, 2 * channels)).astype(BF16)
        v_v[part, :] = dot(fa[i], weight(2 * channels, 3 * channels)).astype(BF16)
    g_v[...] = contract_cols(h_v[...], weight(3 * channels, 4 * channels)).astype(BF16)

    head_size = channels // HEADS
    scale = head_size ** (-0.5)
    log2e = 1.4426950408889634
    lane = lax.broadcasted_iota(jnp.int32, (1, PAIR), 1)
    masks = [jnp.where(lane < head_size, 1.0, 0.0).astype(BF16), jnp.where(lane < head_size, 0.0, 1.0).astype(BF16)]
    chunks = [reds[9 * i : 9 * i + 9] for i in range(pairs + 1)]
    flights = [{} for _ in chunks]

    def spread(ch, lo, value):
        term = chunks[ch][0]
        value = value.astype(BF16)
        hi = lo + value.shape[1]
        for i in range(4 * peers):
            cc, yy, xx, zz = i % 2, i // 2 % 2, i // 4 % 2, i // 8
            term[cc, yy, xx, zz, :, lo:hi] = value[i * STRIP : (i + 1) * STRIP, :]

    def sem(ch, i):
        return red_s.at[ch, i], red_r.at[ch, i]

    def stage1(ch):
        term, r1 = chunks[ch][0], chunks[ch][1]
        flights[ch][1] = send(term.at[1 - c], r1, *sem(ch, 0), across_c)

    def stage2(ch):
        term, r1, s1, r2 = chunks[ch][:4]
        flights[ch][1].wait_recv()
        s1[...] = (term[c].astype(F32) + r1[...].astype(F32)).astype(BF16)
        flights[ch][2] = send(s1.at[1 - y], r2, *sem(ch, 1), across_y)

    def stage3(ch):
        s1, r2, s2, r3 = chunks[ch][2:6]
        flights[ch][2].wait_recv()
        s2[...] = (s1[y].astype(F32) + r2[...].astype(F32)).astype(BF16)
        flights[ch][3] = send(s2.at[1 - x], r3, *sem(ch, 2), across_x)

    def stage4(ch):
        s2, r3, s3, r4 = chunks[ch][4:8]
        flights[ch][3].wait_recv()
        s3[...] = (s2[x].astype(F32) + r3[...].astype(F32)).astype(BF16)
        flights[ch][4] = []
        for k in range(1, zs):
            zz = lax.rem(z + k, zs)
            flights[ch][4].append(send(s3.at[zz], r4.at[k - 1], *sem(ch, 2 + k), (zz * 2 + x, p)))

    def stage5(ch):
        s3, r4, full = chunks[ch][6:9]
        total = s3[z].astype(F32)
        for k in range(1, zs):
            flights[ch][4][k - 1].wait_recv()
            total = total + r4[k - 1].astype(F32)
        full[p] = total.astype(BF16)
        flights[ch][5] = []
        for k in range(1, 4):
            flights[ch][5].append(send(full.at[p], full.at[p], *sem(ch, 2 + zs - 1 + k), (r, lax.rem(p + k, 4))))

    def stage6(ch):
        full = chunks[ch][8]
        for copy in flights[ch][5]:
            copy.wait_recv()
        value = full[...].astype(F32).reshape(4 * STRIP, full.shape[2])
        if ch < pairs:
            for i in range(3):
                lo = i * channels + ch * PAIR
                qg_ref[:, lo : lo + PAIR] = value[:, i * PAIR : (i + 1) * PAIR]
        else:
            pg_ref[...] = value

    stages = [stage1, stage2, stage3, stage4, stage5, stage6]

    def tick(t):
        for i, stage in enumerate(stages):
            if 0 <= t - i <= pairs:
                stage(t - i)

    dk_copies = []
    for hp in range(pairs):
        cols = slice(hp * PAIR, (hp + 1) * PAIR)
        qp, kp, vp, gp = q_v[:, cols], k_v[:, cols], v_v[:, cols], g_v[:, cols]
        k_t = kp.astype(F32).T.astype(BF16)
        v_t = vp.astype(F32).T.astype(BF16)
        dk = dv = None
        dq_t = []
        for e in range(2):
            mine = slice(e * head_size, (e + 1) * head_size)
            qm, gm = qp * masks[e], gp * masks[e]
            score = contract_cols(kp, qm)
            raised = jnp.exp2((score - jnp.max(score, axis=0, keepdims=True)) * (scale * log2e))
            probs = raised * (1.0 / jnp.sum(raised, axis=0, keepdims=True))
            probs_b = probs.astype(BF16)
            dprob = contract_cols(vp, gm)
            delta = jnp.sum(probs * dprob, axis=0, keepdims=True)
            dscore = (probs * (dprob - delta)).astype(BF16)
            at_v[hp * PAIR + e * head_size : hp * PAIR + (e + 1) * head_size, :] = dot(v_t[mine], probs_b).astype(BF16)
            dq_t.append(dot(k_t[mine], dscore))
            dk_e, dv_e = dot(dscore, qm), dot(probs_b, gm)
            dk = dk_e if dk is None else dk + dk_e
            dv = dv_e if dv is None else dv + dv_e
        dq_b = (jnp.concatenate(dq_t, axis=0) * scale).T.astype(BF16)
        dk = dk * scale
        dk_b, dv_b = dk.astype(BF16), dv.astype(BF16)
        dks[hp, 0] = dk_b[rows:]
        dks[hp, 1] = dv_b[rows:]
        dk_copies.append(send(dks.at[hp], dkr.at[hp], dk_s.at[hp], dk_r.at[hp], across_x))
        dq_v[:, cols] = dq_b
        dk_v[:, cols] = dk[:rows]
        dv_v[:, cols] = dv[:rows]
        spread(hp, 0, dot(ft[:, 0:rows], dq_b))
        spread(hp, PAIR, dot(ft[...], dk_b))
        spread(hp, 2 * PAIR, dot(ft[...], dv_b))
        tick(hp)
    spread(pairs, 0, dot(at_v[...], h_v[...]))
    tick(pairs)
    hfeat = contract_cols(dq_v[...], weight(0, channels))
    for hp in range(pairs):
        cols = slice(hp * PAIR, (hp + 1) * PAIR)
        dk_copies[hp].wait_recv()
        dk_v[:, cols] = dk_v[:, cols] + dkr[hp, 0].astype(F32)
        dv_v[:, cols] = dv_v[:, cols] + dkr[hp, 1].astype(F32)
    hfeat = hfeat + contract_cols(dk_v[...].astype(BF16), weight(channels, 2 * channels))
    hfeat = hfeat + contract_cols(dv_v[...].astype(BF16), weight(2 * channels, 3 * channels))
    place = jnp.where(slot_ids == rrow_ref[...], 1.0, 0.0).astype(BF16)
    back_buf[...] = dot(place, hfeat.astype(BF16)).astype(BF16).reshape(peers, per_peer, channels)
    ret_buf[r] = back_buf[r]
    back_copies = []
    for k in range(1, peers):
        d = lax.rem(r + k, peers)
        back_copies.append(send(back_buf.at[d], ret_buf.at[r], bk_s.at[k - 1], bk_r.at[k - 1], (d, p)))
    for t in range(pairs + 1, pairs + 4):
        tick(t)
    for copy in back_copies:
        copy.wait_recv()
    pack = jnp.where(slot_ids == srow_ref[...], 1.0, 0.0).astype(BF16)
    gf_ref[...] = contract_rows(pack, ret_buf[...].reshape(slot_rows, channels)).astype(BF16)
    for t in range(pairs + 4, pairs + len(stages)):
        tick(t)
    for copy in sends:
        copy.wait_send()


def per_device(feats, grad_out, qkv_weight, proj_weight, to_hilbert, to_zorder):
    peers = lax.axis_size("rows")
    feature = feats[0]
    rows, channels = feature.shape
    blocks = to_hilbert.shape[1]
    block = rows // blocks
    forward_list, inverse_list = to_hilbert[0], to_zorder[0]
    target = forward_list // blocks
    send_slot = target * CAP + rank_within(jnp.arange(blocks, dtype=jnp.int32), target)
    source = inverse_list // blocks
    recv_slot = source * CAP + rank_within(inverse_list, source)
    within = jnp.arange(block, dtype=jnp.int32)
    srow = (send_slot[:, None] * block + within[None, :]).reshape(1, rows)
    rrow = (recv_slot[:, None] * block + within[None, :]).reshape(1, rows)
    slot_rows = peers * CAP * block
    zs = peers // 2
    pairs = channels // PAIR
    wide = qkv_weight.shape[1] + channels
    dma = pltpu.SemaphoreType.DMA

    def vm(*shape, kind=BF16):
        return pltpu.VMEM(shape, kind)

    scratch = [
        vm(peers, 4, STRIP, wide),
        dma((zs - 1,)), dma((zs - 1,)), dma((zs,)), dma((zs,)),
        dma((peers - 1,)), dma((peers - 1,)), dma((2 * peers - 2,)), dma((2 * peers - 2,)),
        vm(peers, slot_rows // peers, channels), vm(peers, slot_rows // peers, channels),
        dma((peers - 1,)), dma((peers - 1,)),
        vm(peers, slot_rows // peers, channels), vm(peers, slot_rows // peers, channels),
        dma((peers - 1,)), dma((peers - 1,)),
        vm(2, rows, channels), vm(channels, 2 * rows), dma, dma,
        vm(rows, channels), vm(2 * rows, channels), vm(2 * rows, channels), vm(rows, channels), vm(rows, channels),
        vm(channels, rows), vm(rows, channels), vm(rows, channels, kind=F32), vm(rows, channels, kind=F32),
        vm(pairs, 2, rows, PAIR), vm(pairs, 2, rows, PAIR), dma((pairs,)), dma((pairs,)),
        dma((pairs + 1, zs + 5)), dma((pairs + 1, zs + 5)),
    ]
    for ch in range(pairs + 1):
        w = 3 * PAIR if ch < pairs else channels
        scratch += [vm(2, 2, 2, zs, STRIP, w), vm(2, 2, zs, STRIP, w), vm(2, 2, zs, STRIP, w),
                    vm(2, zs, STRIP, w), vm(2, zs, STRIP, w), vm(zs, STRIP, w), vm(zs, STRIP, w),
                    vm(zs - 1, STRIP, w), vm(4, STRIP, w)]

    def body(*refs):
        fused_kernel(peers, slot_rows, *refs)

    share = qkv_weight.shape[0]
    grad_z, qkv_grad, proj_grad = pl.pallas_call(
        body,
        out_shape=(
            jax.ShapeDtypeStruct((rows, channels), BF16),
            jax.ShapeDtypeStruct((share, qkv_weight.shape[1]), F32),
            jax.ShapeDtypeStruct((share, channels), F32),
        ),
        in_specs=[pl.BlockSpec(memory_space=pltpu.VMEM)] * 6,
        out_specs=(pl.BlockSpec(memory_space=pltpu.VMEM),) * 3,
        scratch_shapes=scratch,
        compiler_params=pltpu.CompilerParams(
            collective_id=0, has_side_effects=True, vmem_limit_bytes=48 * 1024 * 1024
        ),
    )(feature, grad_out[0], qkv_weight, proj_weight, srow, rrow)
    return grad_z[None], qkv_grad, proj_grad


def fits_kernel(mesh):
    return mesh.shape["rows"] == 8 and mesh.shape["rep"] == 4


def solution(mesh):
    placed = (
        P("rep", "rows", None),
        P("rep", "rows", None),
        P("rows", None),
        P("rows", None),
        P("rep", "rows"),
        P("rep", "rows"),
    )
    return jax.shard_map(
        per_device if fits_kernel(mesh) else per_device_general,
        mesh=mesh,
        in_specs=placed,
        out_specs=(P("rep", "rows", None), P("rows", None), P("rows", None)),
        check_vma=False,
    )
```

```python
import jax
import jax.numpy as jnp
from jax import lax
from jax.experimental import pallas as pl
from jax.experimental.pallas import tpu as pltpu
from jax.sharding import PartitionSpec as P

HEADS = 8
CAP = 2


def from_partner(block, axis, apart):
    count = lax.axis_size(axis)
    route = []
    for low in range(count):
        high = low | 1 << apart
        if high != low and high < count:
            route += [(low, high), (high, low)]
    return lax.ppermute(block, axis, route)


def move_blocks(outgoing):
    return lax.all_to_all(outgoing, "rows", split_axis=0, concat_axis=0, tiled=True)


def rank_within(order_keys, owners):
    same_owner = owners[None, :] == owners[:, None]
    earlier = order_keys[None, :] < order_keys[:, None]
    return jnp.sum(jnp.logical_and(same_owner, earlier).astype(jnp.int32), axis=1)


def contract_rows(left, right):
    return lax.dot_general(
        left, right, (((0,), (0,)), ((), ())), preferred_element_type=jnp.float32
    )


def contract_cols(left, right):
    return lax.dot_general(
        left, right, (((1,), (1,)), ((), ())), preferred_element_type=jnp.float32
    )


def per_device_general(feats, grad_out, qkv_weight, proj_weight, to_hilbert, to_zorder):
    peer_count = lax.axis_size("rows")
    feature = feats[0]
    rows_dev, channels = feature.shape
    head_size = channels // HEADS
    scale = head_size ** (-0.5)
    blocks_dev = to_hilbert.shape[1]
    slot_count = peer_count * CAP
    w_qkv, w_proj = (
        lax.all_gather(qkv_weight, "rows", axis=0, tiled=True),
        lax.all_gather(proj_weight, "rows", axis=0, tiled=True),
    )
    forward_list = to_hilbert[0]
    inverse_list = to_zorder[0]
    local_ids = jnp.arange(blocks_dev, dtype=jnp.int32)
    slot_ids = jnp.arange(slot_count, dtype=jnp.int32)
    target_dev = forward_list // blocks_dev
    send_slot = target_dev * CAP + rank_within(local_ids, target_dev)
    send_table = (send_slot[None, :] == slot_ids[:, None]).astype(jnp.bfloat16)
    source_dev = inverse_list // blocks_dev
    recv_slot = source_dev * CAP + rank_within(inverse_list, source_dev)
    recv_table = (recv_slot[:, None] == slot_ids[None, :]).astype(jnp.bfloat16)
    zblocks = grad_out[0].reshape(blocks_dev, -1)
    outgoing = jnp.dot(send_table, zblocks, preferred_element_type=jnp.float32).astype(jnp.bfloat16)
    arrived = move_blocks(outgoing.reshape(peer_count, CAP, -1)).reshape(slot_count, -1)
    grad_hil = jnp.dot(recv_table, arrived, preferred_element_type=jnp.float32).astype(jnp.bfloat16)
    grad_hil = grad_hil.reshape(rows_dev, channels)
    qkv = jnp.dot(feature, w_qkv, preferred_element_type=jnp.float32).astype(jnp.bfloat16)
    query = qkv[:, :channels]
    keyval = qkv[:, channels:]
    grad_attn = contract_cols(grad_hil, w_proj).astype(jnp.bfloat16)
    other_kv = from_partner(keyval, "rows", 0)
    keys_all = jnp.concatenate([keyval[:, :channels], other_kv[:, :channels]], axis=0)
    values_all = jnp.concatenate([keyval[:, channels:], other_kv[:, channels:]], axis=0)
    attn_parts, dq_parts, dk_parts, dv_parts = ([], [], [], [])
    for head_index in range(HEADS):
        lo_col = head_index * head_size
        q_head = query[:, lo_col : lo_col + head_size]
        k_head = keys_all[:, lo_col : lo_col + head_size]
        v_head = values_all[:, lo_col : lo_col + head_size]
        g_head = grad_attn[:, lo_col : lo_col + head_size]
        score = contract_cols(q_head, k_head) * scale
        row_max = jnp.max(score, axis=1, keepdims=True)
        raised = jnp.exp(score - row_max)
        row_sum = jnp.sum(raised, axis=1, keepdims=True)
        probs = raised / row_sum
        probs_b = probs.astype(jnp.bfloat16)
        attn_parts.append(
            jnp.dot(probs_b, v_head, preferred_element_type=jnp.float32).astype(jnp.bfloat16)
        )
        dprob = contract_cols(g_head, v_head)
        delta = jnp.sum(probs * dprob, axis=1, keepdims=True)
        dscore = (probs * (dprob - delta) * scale).astype(jnp.bfloat16)
        dq_parts.append(jnp.dot(dscore, k_head, preferred_element_type=jnp.float32))
        dk_parts.append(contract_rows(dscore, q_head))
        dv_parts.append(contract_rows(probs_b, g_head))
    grad_q = jnp.concatenate(dq_parts, axis=1)
    grad_k = jnp.concatenate(dk_parts, axis=1)
    grad_v = jnp.concatenate(dv_parts, axis=1)
    other_k, other_v = (
        from_partner(grad_k[rows_dev:].astype(jnp.bfloat16), "rows", 0).astype(jnp.float32),
        from_partner(grad_v[rows_dev:].astype(jnp.bfloat16), "rows", 0).astype(jnp.float32),
    )
    grad_k = grad_k[:rows_dev] + other_k
    grad_v = grad_v[:rows_dev] + other_v
    grad_qkv = jnp.concatenate([grad_q, grad_k, grad_v], axis=1).astype(jnp.bfloat16)
    attn = jnp.concatenate(attn_parts, axis=1)
    grad_hfeat = contract_cols(grad_qkv, w_qkv).astype(jnp.bfloat16)
    hblocks = grad_hfeat.reshape(blocks_dev, -1)
    going_back = contract_rows(recv_table, hblocks).astype(jnp.bfloat16)
    returned = move_blocks(going_back.reshape(peer_count, CAP, -1)).reshape(slot_count, -1)
    grad_z = contract_rows(send_table, returned).astype(jnp.bfloat16).reshape(rows_dev, channels)
    share = channels // peer_count
    term = jnp.concatenate(
        [contract_rows(feature, grad_qkv), contract_rows(attn, grad_hil)], axis=1
    )
    total = lax.psum(term, ("rows", "rep"))
    owned = lax.dynamic_slice_in_dim(total, lax.axis_index("rows") * share, share, 0)
    return (grad_z[None], owned[:, : 3 * channels], owned[:, 3 * channels :])


MESH = pl.DeviceIdType.MESH
PAIR = 128
STRIP = 16
F32 = jnp.float32
BF16 = jnp.bfloat16


def dot(left, right):
    return jnp.dot(left, right, preferred_element_type=F32)


def slot_of_row(owners, order_keys, block, rows):
    lane = lax.broadcasted_iota(jnp.int32, (1, rows), 1)
    out = lax.rem(lane, block)
    for i, owner in enumerate(owners):
        rank = jnp.int32(0)
        for j, other in enumerate(owners):
            if j != i:
                rank += jnp.where(jnp.logical_and(other == owner, order_keys[j] < order_keys[i]), 1, 0)
        out += jnp.where(lax.div(lane, block) == i, (owner * CAP + rank) * block, 0)
    return out


def fused_kernel(peers, slot_rows, feats_hbm, grad_hbm, wq_hbm, wp_hbm, toh_hbm, toz_hbm,
                 gf_ref, qg_ref, pg_ref,
                 wf, wz_s, wz_r, wx_s, wx_r, wy_s, wy_r, wc_s, wc_r,
                 out_buf, arr_buf, sl_s, sl_r, back_buf, ret_buf, bk_s, bk_r,
                 fa, ft, ff_s, ff_r, q_v, k_v, v_v, g_v, h_v, at_v, dq_v, dk_v, dv_v,
                 dks, dkr, dk_s, dk_r, red_s, red_r, grad_v, toh, toz, in_sem, probs_v, *reds):
    rows, channels = feats_hbm.shape
    blocks = toh_hbm.shape[1]
    pairs = channels // PAIR
    r = lax.axis_index("rows")
    p = lax.axis_index("rep")
    x, z = lax.rem(r, 2), lax.div(r, 2)
    c, y = lax.rem(p, 2), lax.div(p, 2)
    across_x = (r + 1 - 2 * x, p)
    across_c = (r, p + 1 - 2 * c)
    across_y = (r, p + 2 - 4 * y)
    zs = peers // 2
    sends = []

    def send(src, dst, send_sem, recv_sem, device):
        copy = pltpu.make_async_remote_copy(
            src_ref=src, dst_ref=dst, send_sem=send_sem, recv_sem=recv_sem,
            device_id=device, device_id_type=MESH)
        copy.start()
        sends.append(copy)
        return copy

    wide = wq_hbm.shape[2]
    loads = []
    for i, (src, dst) in enumerate([(toh_hbm, toh), (toz_hbm, toz), (grad_hbm, grad_v),
                                    (wq_hbm, wf.at[r, :, :, pl.ds(0, wide)]),
                                    (wp_hbm, wf.at[r, :, :, pl.ds(wide, channels)]),
                                    (feats_hbm, fa.at[0])]):
        copy = pltpu.make_async_copy(src, dst, in_sem.at[i])
        copy.start()
        loads.append(copy)
    barrier = pltpu.get_barrier_semaphore()
    for k in range(1, peers):
        pl.semaphore_signal(barrier, inc=1, device_id=(lax.rem(r + k, peers), p), device_id_type=MESH)
    for k in range(1, 4):
        pl.semaphore_signal(barrier, inc=1, device_id=(r, lax.rem(p + k, 4)), device_id_type=MESH)

    for copy in loads[:2]:
        copy.wait()
    forward_list = [toh[0, i] for i in range(blocks)]
    inverse_list = [toz[0, i] for i in range(blocks)]
    srow = slot_of_row([lax.div(b, blocks) for b in forward_list], list(range(blocks)), rows // blocks, rows)
    rrow = slot_of_row([lax.div(b, blocks) for b in inverse_list], inverse_list, rows // blocks, rows)
    slot_ids = lax.broadcasted_iota(jnp.int32, (slot_rows, rows), 0)
    pack = jnp.where(slot_ids == srow, 1.0, 0.0).astype(BF16)
    per_peer = slot_rows // peers
    loads[2].wait()
    out_buf[...] = dot(pack, grad_v[...]).astype(BF16).reshape(peers, per_peer, channels)
    arr_buf[r] = out_buf[r]
    for copy in loads[3:]:
        copy.wait()
    pl.semaphore_wait(barrier, peers - 1 + 3)

    z_copies = []
    for k in range(1, zs):
        to = (lax.rem(z + k, zs) * 2 + x, p)
        z_copies.append(send(wf.at[r, p], wf.at[r, p], wz_s.at[k - 1], wz_r.at[k - 1], to))
    x_copies = [send(wf.at[r, p], wf.at[r, p], wx_s.at[0], wx_r.at[0], across_x)]
    f_copy = send(fa.at[0], fa.at[1], ff_s, ff_r, across_x)
    y_copies, c_copies = [], []

    def to_y(row):
        i = len(y_copies)
        y_copies.append((send(wf.at[row, p], wf.at[row, p], wy_s.at[i], wy_r.at[i], across_y), row))

    def to_c(row, strip):
        i = len(c_copies)
        c_copies.append(send(wf.at[row, strip], wf.at[row, strip], wc_s.at[i], wc_r.at[i], across_c))

    for k in range(1, zs):
        z_copies[k - 1].wait_recv()
        row = lax.rem(z + zs - k, zs) * 2 + x
        x_copies.append(send(wf.at[row, p], wf.at[row, p], wx_s.at[k], wx_r.at[k], across_x))
        to_y(row)
        to_c(row, p)
    slot_copies = []
    for k in range(1, peers):
        d = lax.rem(r + k, peers)
        slot_copies.append(send(out_buf.at[d], arr_buf.at[r], sl_s.at[k - 1], sl_r.at[k - 1], (d, p)))
    for k in range(zs):
        x_copies[k].wait_recv()
        row = lax.rem(z + zs - k, zs) * 2 + 1 - x
        to_y(row)
        to_c(row, p)
    f_copy.wait_recv()
    for i in range(2):
        ft[:, i * rows : (i + 1) * rows] = fa[i].astype(F32).T.astype(BF16)
    for copy, row in y_copies:
        copy.wait_recv()
        to_c(row, p + 2 - 4 * y)
    for copy in c_copies:
        copy.wait_recv()

    def weight(lo, hi):
        return wf[:, :, :, lo:hi].reshape(4 * STRIP * peers, hi - lo)

    q_v[...] = dot(fa[0], weight(0, channels)).astype(BF16)
    for i in range(2):
        part = slice(i * rows, (i + 1) * rows)
        k_v[part, :] = dot(fa[i], weight(channels, 2 * channels)).astype(BF16)
        v_v[part, :] = dot(fa[i], weight(2 * channels, 3 * channels)).astype(BF16)

    head_size = channels // HEADS
    scale = head_size ** (-0.5)
    log2e = 1.4426950408889634
    lane = lax.broadcasted_iota(jnp.int32, (1, PAIR), 1)
    masks = [jnp.where(lane < head_size, 1.0, 0.0).astype(BF16), jnp.where(lane < head_size, 0.0, 1.0).astype(BF16)]
    chunks = [reds[9 * i : 9 * i + 9] for i in range(pairs + 1)]
    flights = [{} for _ in chunks]

    def spread(ch, lo, value):
        term = chunks[ch][0]
        value = value.astype(BF16)
        hi = lo + value.shape[1]
        for i in range(4 * peers):
            cc, yy, xx, zz = i % 2, i // 2 % 2, i // 4 % 2, i // 8
            term[cc, yy, xx, zz, :, lo:hi] = value[i * STRIP : (i + 1) * STRIP, :]

    def sem(ch, i):
        return red_s.at[ch, i], red_r.at[ch, i]

    def stage1(ch):
        term, r1 = chunks[ch][0], chunks[ch][1]
        flights[ch][1] = send(term.at[1 - c], r1, *sem(ch, 0), across_c)

    def stage2(ch):
        term, r1, s1, r2 = chunks[ch][:4]
        flights[ch][1].wait_recv()
        s1[...] = (term[c].astype(F32) + r1[...].astype(F32)).astype(BF16)
        flights[ch][2] = send(s1.at[1 - y], r2, *sem(ch, 1), across_y)

    def stage3(ch):
        s1, r2, s2, r3 = chunks[ch][2:6]
        flights[ch][2].wait_recv()
        s2[...] = (s1[y].astype(F32) + r2[...].astype(F32)).astype(BF16)
        flights[ch][3] = send(s2.at[1 - x], r3, *sem(ch, 2), across_x)

    def stage4(ch):
        s2, r3, s3, r4 = chunks[ch][4:8]
        flights[ch][3].wait_recv()
        s3[...] = (s2[x].astype(F32) + r3[...].astype(F32)).astype(BF16)
        flights[ch][4] = []
        for k in range(1, zs):
            zz = lax.rem(z + k, zs)
            flights[ch][4].append(send(s3.at[zz], r4.at[k - 1], *sem(ch, 2 + k), (zz * 2 + x, p)))

    def stage5(ch):
        s3, r4, full = chunks[ch][6:9]
        total = s3[z].astype(F32)
        for k in range(1, zs):
            flights[ch][4][k - 1].wait_recv()
            total = total + r4[k - 1].astype(F32)
        full[p] = total.astype(BF16)
        flights[ch][5] = []
        for k in range(1, 4):
            flights[ch][5].append(send(full.at[p], full.at[p], *sem(ch, 2 + zs - 1 + k), (r, lax.rem(p + k, 4))))

    def stage6(ch):
        full = chunks[ch][8]
        for copy in flights[ch][5]:
            copy.wait_recv()
        value = full[...].astype(F32).reshape(4 * STRIP, full.shape[2])
        if ch > 0:
            for i in range(3):
                lo = i * channels + (ch - 1) * PAIR
                qg_ref[:, lo : lo + PAIR] = value[:, i * PAIR : (i + 1) * PAIR]
        else:
            pg_ref[...] = value

    stages = [stage1, stage2, stage3, stage4, stage5, stage6]

    def tick(t):
        for i, stage in enumerate(stages):
            if 0 <= t - i <= pairs:
                stage(t - i)

    for hp in range(pairs):
        cols = slice(hp * PAIR, (hp + 1) * PAIR)
        qp, kp = q_v[:, cols], k_v[:, cols]
        v_t = v_v[:, cols].astype(F32).T.astype(BF16)
        for e in range(2):
            mine = slice(e * head_size, (e + 1) * head_size)
            score = contract_cols(kp, qp * masks[e])
            raised = jnp.exp2((score - jnp.max(score, axis=0, keepdims=True)) * (scale * log2e))
            probs = raised * (1.0 / jnp.sum(raised, axis=0, keepdims=True))
            probs_v[2 * hp + e] = probs
            at_v[hp * PAIR + e * head_size : hp * PAIR + (e + 1) * head_size, :] = dot(
                v_t[mine], probs.astype(BF16)).astype(BF16)

    for copy in slot_copies:
        copy.wait_recv()
    place = jnp.where(slot_ids == rrow, 1.0, 0.0).astype(BF16)
    h_v[...] = contract_rows(place, arr_buf[...].reshape(slot_rows, channels)).astype(BF16)
    spread(0, 0, dot(at_v[...], h_v[...]))
    tick(0)
    g_v[...] = contract_cols(h_v[...], weight(3 * channels, 4 * channels)).astype(BF16)

    dk_copies = []
    for hp in range(pairs):
        cols = slice(hp * PAIR, (hp + 1) * PAIR)
        qp, kp, vp, gp = q_v[:, cols], k_v[:, cols], v_v[:, cols], g_v[:, cols]
        k_t = kp.astype(F32).T.astype(BF16)
        dk = dv = None
        dq_t = []
        for e in range(2):
            mine = slice(e * head_size, (e + 1) * head_size)
            qm, gm = qp * masks[e], gp * masks[e]
            probs = probs_v[2 * hp + e]
            probs_b = probs.astype(BF16)
            dprob = contract_cols(vp, gm)
            delta = jnp.sum(probs * dprob, axis=0, keepdims=True)
            dscore = (probs * (dprob - delta)).astype(BF16)
            dq_t.append(dot(k_t[mine], dscore))
            dk_e, dv_e = dot(dscore, qm), dot(probs_b, gm)
            dk = dk_e if dk is None else dk + dk_e
            dv = dv_e if dv is None else dv + dv_e
        dq_b = (jnp.concatenate(dq_t, axis=0) * scale).T.astype(BF16)
        dk = dk * scale
        dk_b, dv_b = dk.astype(BF16), dv.astype(BF16)
        dks[hp, 0] = dk_b[rows:]
        dks[hp, 1] = dv_b[rows:]
        dk_copies.append(send(dks.at[hp], dkr.at[hp], dk_s.at[hp], dk_r.at[hp], across_x))
        dq_v[:, cols] = dq_b
        dk_v[:, cols] = dk[:rows]
        dv_v[:, cols] = dv[:rows]
        spread(1 + hp, 0, dot(ft[:, 0:rows], dq_b))
        spread(1 + hp, PAIR, dot(ft[...], dk_b))
        spread(1 + hp, 2 * PAIR, dot(ft[...], dv_b))
        tick(1 + hp)
    hfeat = contract_cols(dq_v[...], weight(0, channels))
    for lo, hi in ((0, pairs - 1), (pairs - 1, pairs)):
        part = slice(lo * PAIR, hi * PAIR)
        for hp in range(lo, hi):
            cols = slice(hp * PAIR, (hp + 1) * PAIR)
            dk_copies[hp].wait_recv()
            dk_v[:, cols] = dk_v[:, cols] + dkr[hp, 0].astype(F32)
            dv_v[:, cols] = dv_v[:, cols] + dkr[hp, 1].astype(F32)
        hfeat += contract_cols(dk_v[:, part].astype(BF16), weight(channels + lo * PAIR, channels + hi * PAIR))
        hfeat += contract_cols(dv_v[:, part].astype(BF16), weight(2 * channels + lo * PAIR, 2 * channels + hi * PAIR))
    place = jnp.where(slot_ids == rrow, 1.0, 0.0).astype(BF16)
    back_buf[...] = dot(place, hfeat.astype(BF16)).astype(BF16).reshape(peers, per_peer, channels)
    ret_buf[r] = back_buf[r]
    back_copies = []
    for k in range(1, peers):
        d = lax.rem(r + k, peers)
        back_copies.append(send(back_buf.at[d], ret_buf.at[r], bk_s.at[k - 1], bk_r.at[k - 1], (d, p)))
    for t in range(pairs + 1, pairs + 4):
        tick(t)
    for copy in back_copies:
        copy.wait_recv()
    pack = jnp.where(slot_ids == srow, 1.0, 0.0).astype(BF16)
    gf_ref[...] = contract_rows(pack, ret_buf[...].reshape(slot_rows, channels)).astype(BF16)
    for t in range(pairs + 4, pairs + len(stages)):
        tick(t)
    for copy in sends:
        copy.wait_send()


def per_device(feats, grad_out, qkv_weight, proj_weight, to_hilbert, to_zorder):
    peers = lax.axis_size("rows")
    feature = feats[0]
    rows, channels = feature.shape
    blocks = to_hilbert.shape[1]
    block = rows // blocks
    slot_rows = peers * CAP * block
    zs = peers // 2
    pairs = channels // PAIR
    wide = qkv_weight.shape[1] + channels
    dma = pltpu.SemaphoreType.DMA

    def vm(*shape, kind=BF16):
        return pltpu.VMEM(shape, kind)

    scratch = [
        vm(peers, 4, STRIP, wide),
        dma((zs - 1,)), dma((zs - 1,)), dma((zs,)), dma((zs,)),
        dma((peers - 1,)), dma((peers - 1,)), dma((2 * peers - 2,)), dma((2 * peers - 2,)),
        vm(peers, slot_rows // peers, channels), vm(peers, slot_rows // peers, channels),
        dma((peers - 1,)), dma((peers - 1,)),
        vm(peers, slot_rows // peers, channels), vm(peers, slot_rows // peers, channels),
        dma((peers - 1,)), dma((peers - 1,)),
        vm(2, rows, channels), vm(channels, 2 * rows), dma, dma,
        vm(rows, channels), vm(2 * rows, channels), vm(2 * rows, channels), vm(rows, channels), vm(rows, channels),
        vm(channels, rows), vm(rows, channels), vm(rows, channels, kind=F32), vm(rows, channels, kind=F32),
        vm(pairs, 2, rows, PAIR), vm(pairs, 2, rows, PAIR), dma((pairs,)), dma((pairs,)),
        dma((pairs + 1, zs + 5)), dma((pairs + 1, zs + 5)),
        vm(rows, channels), pltpu.SMEM((1, blocks), jnp.int32), pltpu.SMEM((1, blocks), jnp.int32), dma((6,)),
        vm(HEADS, 2 * rows, rows, kind=F32),
    ]
    for ch in range(pairs + 1):
        w = 3 * PAIR if ch > 0 else channels
        scratch += [vm(2, 2, 2, zs, STRIP, w), vm(2, 2, zs, STRIP, w), vm(2, 2, zs, STRIP, w),
                    vm(2, zs, STRIP, w), vm(2, zs, STRIP, w), vm(zs, STRIP, w), vm(zs, STRIP, w),
                    vm(zs - 1, STRIP, w), vm(4, STRIP, w)]

    def body(*refs):
        fused_kernel(peers, slot_rows, *refs)

    share = qkv_weight.shape[0]
    grad_z, qkv_grad, proj_grad = pl.pallas_call(
        body,
        out_shape=(
            jax.ShapeDtypeStruct((rows, channels), BF16),
            jax.ShapeDtypeStruct((share, qkv_weight.shape[1]), F32),
            jax.ShapeDtypeStruct((share, channels), F32),
        ),
        in_specs=[pl.BlockSpec(memory_space=pltpu.HBM)] * 6,
        out_specs=(pl.BlockSpec(memory_space=pltpu.VMEM),) * 3,
        scratch_shapes=scratch,
        compiler_params=pltpu.CompilerParams(
            collective_id=0, has_side_effects=True, vmem_limit_bytes=48 * 1024 * 1024
        ),
    )(feature, grad_out[0], qkv_weight.reshape(4, STRIP, -1), proj_weight.reshape(4, STRIP, -1), to_hilbert, to_zorder)
    return grad_z[None], qkv_grad, proj_grad


def fits_kernel(mesh):
    return mesh.shape["rows"] == 8 and mesh.shape["rep"] == 4


def solution(mesh):
    placed = (
        P("rep", "rows", None),
        P("rep", "rows", None),
        P("rows", None),
        P("rows", None),
        P("rep", "rows"),
        P("rep", "rows"),
    )
    return jax.shard_map(
        per_device if fits_kernel(mesh) else per_device_general,
        mesh=mesh,
        in_specs=placed,
        out_specs=(P("rep", "rows", None), P("rows", None), P("rows", None)),
        check_vma=False,
    )
```

```python
import jax
import jax.numpy as jnp
from jax import lax
from jax.experimental import pallas as pl
from jax.experimental.pallas import tpu as pltpu
from jax.sharding import PartitionSpec as P

HEADS = 8
CAP = 2


def from_partner(block, axis, apart):
    count = lax.axis_size(axis)
    route = []
    for low in range(count):
        high = low | 1 << apart
        if high != low and high < count:
            route += [(low, high), (high, low)]
    return lax.ppermute(block, axis, route)


def move_blocks(outgoing):
    return lax.all_to_all(outgoing, "rows", split_axis=0, concat_axis=0, tiled=True)


def rank_within(order_keys, owners):
    same_owner = owners[None, :] == owners[:, None]
    earlier = order_keys[None, :] < order_keys[:, None]
    return jnp.sum(jnp.logical_and(same_owner, earlier).astype(jnp.int32), axis=1)


def contract_rows(left, right):
    return lax.dot_general(
        left, right, (((0,), (0,)), ((), ())), preferred_element_type=jnp.float32
    )


def contract_cols(left, right):
    return lax.dot_general(
        left, right, (((1,), (1,)), ((), ())), preferred_element_type=jnp.float32
    )


def per_device_general(feats, grad_out, qkv_weight, proj_weight, to_hilbert, to_zorder):
    peer_count = lax.axis_size("rows")
    feature = feats[0]
    rows_dev, channels = feature.shape
    head_size = channels // HEADS
    scale = head_size ** (-0.5)
    blocks_dev = to_hilbert.shape[1]
    slot_count = peer_count * CAP
    w_qkv, w_proj = (
        lax.all_gather(qkv_weight, "rows", axis=0, tiled=True),
        lax.all_gather(proj_weight, "rows", axis=0, tiled=True),
    )
    forward_list = to_hilbert[0]
    inverse_list = to_zorder[0]
    local_ids = jnp.arange(blocks_dev, dtype=jnp.int32)
    slot_ids = jnp.arange(slot_count, dtype=jnp.int32)
    target_dev = forward_list // blocks_dev
    send_slot = target_dev * CAP + rank_within(local_ids, target_dev)
    send_table = (send_slot[None, :] == slot_ids[:, None]).astype(jnp.bfloat16)
    source_dev = inverse_list // blocks_dev
    recv_slot = source_dev * CAP + rank_within(inverse_list, source_dev)
    recv_table = (recv_slot[:, None] == slot_ids[None, :]).astype(jnp.bfloat16)
    zblocks = grad_out[0].reshape(blocks_dev, -1)
    outgoing = jnp.dot(send_table, zblocks, preferred_element_type=jnp.float32).astype(jnp.bfloat16)
    arrived = move_blocks(outgoing.reshape(peer_count, CAP, -1)).reshape(slot_count, -1)
    grad_hil = jnp.dot(recv_table, arrived, preferred_element_type=jnp.float32).astype(jnp.bfloat16)
    grad_hil = grad_hil.reshape(rows_dev, channels)
    qkv = jnp.dot(feature, w_qkv, preferred_element_type=jnp.float32).astype(jnp.bfloat16)
    query = qkv[:, :channels]
    keyval = qkv[:, channels:]
    grad_attn = contract_cols(grad_hil, w_proj).astype(jnp.bfloat16)
    other_kv = from_partner(keyval, "rows", 0)
    keys_all = jnp.concatenate([keyval[:, :channels], other_kv[:, :channels]], axis=0)
    values_all = jnp.concatenate([keyval[:, channels:], other_kv[:, channels:]], axis=0)
    attn_parts, dq_parts, dk_parts, dv_parts = ([], [], [], [])
    for head_index in range(HEADS):
        lo_col = head_index * head_size
        q_head = query[:, lo_col : lo_col + head_size]
        k_head = keys_all[:, lo_col : lo_col + head_size]
        v_head = values_all[:, lo_col : lo_col + head_size]
        g_head = grad_attn[:, lo_col : lo_col + head_size]
        score = contract_cols(q_head, k_head) * scale
        row_max = jnp.max(score, axis=1, keepdims=True)
        raised = jnp.exp(score - row_max)
        row_sum = jnp.sum(raised, axis=1, keepdims=True)
        probs = raised / row_sum
        probs_b = probs.astype(jnp.bfloat16)
        attn_parts.append(
            jnp.dot(probs_b, v_head, preferred_element_type=jnp.float32).astype(jnp.bfloat16)
        )
        dprob = contract_cols(g_head, v_head)
        delta = jnp.sum(probs * dprob, axis=1, keepdims=True)
        dscore = (probs * (dprob - delta) * scale).astype(jnp.bfloat16)
        dq_parts.append(jnp.dot(dscore, k_head, preferred_element_type=jnp.float32))
        dk_parts.append(contract_rows(dscore, q_head))
        dv_parts.append(contract_rows(probs_b, g_head))
    grad_q = jnp.concatenate(dq_parts, axis=1)
    grad_k = jnp.concatenate(dk_parts, axis=1)
    grad_v = jnp.concatenate(dv_parts, axis=1)
    other_k, other_v = (
        from_partner(grad_k[rows_dev:].astype(jnp.bfloat16), "rows", 0).astype(jnp.float32),
        from_partner(grad_v[rows_dev:].astype(jnp.bfloat16), "rows", 0).astype(jnp.float32),
    )
    grad_k = grad_k[:rows_dev] + other_k
    grad_v = grad_v[:rows_dev] + other_v
    grad_qkv = jnp.concatenate([grad_q, grad_k, grad_v], axis=1).astype(jnp.bfloat16)
    attn = jnp.concatenate(attn_parts, axis=1)
    grad_hfeat = contract_cols(grad_qkv, w_qkv).astype(jnp.bfloat16)
    hblocks = grad_hfeat.reshape(blocks_dev, -1)
    going_back = contract_rows(recv_table, hblocks).astype(jnp.bfloat16)
    returned = move_blocks(going_back.reshape(peer_count, CAP, -1)).reshape(slot_count, -1)
    grad_z = contract_rows(send_table, returned).astype(jnp.bfloat16).reshape(rows_dev, channels)
    share = channels // peer_count
    term = jnp.concatenate(
        [contract_rows(feature, grad_qkv), contract_rows(attn, grad_hil)], axis=1
    )
    total = lax.psum(term, ("rows", "rep"))
    owned = lax.dynamic_slice_in_dim(total, lax.axis_index("rows") * share, share, 0)
    return (grad_z[None], owned[:, : 3 * channels], owned[:, 3 * channels :])


MESH = pl.DeviceIdType.MESH
PAIR = 128
STRIP = 16
F32 = jnp.float32
BF16 = jnp.bfloat16


def dot(left, right):
    return jnp.dot(left, right, preferred_element_type=F32)


def slot_of_row(owners, order_keys, block, rows):
    lane = lax.broadcasted_iota(jnp.int32, (1, rows), 1)
    out = lax.rem(lane, block)
    for i, owner in enumerate(owners):
        rank = jnp.int32(0)
        for j, other in enumerate(owners):
            if j != i:
                rank += jnp.where(jnp.logical_and(other == owner, order_keys[j] < order_keys[i]), 1, 0)
        out += jnp.where(lax.div(lane, block) == i, (owner * CAP + rank) * block, 0)
    return out


def fused_kernel(peers, slot_rows, feats_hbm, grad_hbm, wq_hbm, wp_hbm, toh_hbm, toz_hbm,
                 gf_hbm, qg_hbm, pg_hbm,
                 gf_ref, qg_ref, pg_ref, out_sem, wqf, wpf, wz_s, wz_r, wx_s, wx_r, wy_s, wy_r, wc_s, wc_r,
                 out_buf, arr_buf, sl_s, sl_r, back_buf, ret_buf, bk_s, bk_r,
                 fa, ft, ff_s, ff_r, q_v, k_v, v_v, g_v, h_v, at_v, dq_v, dk_v, dv_v,
                 dks, dkr, dk_s, dk_r, red_s, red_r, grad_v, toh, toz, in_sem, probs_v, *reds):
    rows, channels = feats_hbm.shape
    blocks = toh_hbm.shape[1]
    pairs = channels // PAIR
    r = lax.axis_index("rows")
    p = lax.axis_index("rep")
    x, z = lax.rem(r, 2), lax.div(r, 2)
    c, y = lax.rem(p, 2), lax.div(p, 2)
    across_x = (r + 1 - 2 * x, p)
    across_c = (r, p + 1 - 2 * c)
    across_y = (r, p + 2 - 4 * y)
    zs = peers // 2
    sends = []

    def send(src, dst, send_sem, recv_sem, device):
        copy = pltpu.make_async_remote_copy(
            src_ref=src, dst_ref=dst, send_sem=send_sem, recv_sem=recv_sem,
            device_id=device, device_id_type=MESH)
        copy.start()
        sends.append(copy)
        return copy

    loads = []
    for i, (src, dst) in enumerate([(toh_hbm, toh), (toz_hbm, toz), (grad_hbm, grad_v),
                                    (wq_hbm, wqf.at[r]),
                                    (wp_hbm, wpf.at[r]),
                                    (feats_hbm, fa.at[0])]):
        copy = pltpu.make_async_copy(src, dst, in_sem.at[i])
        copy.start()
        loads.append(copy)
    handed = []

    def hand(src, dst):
        copy = pltpu.make_async_copy(src, dst, out_sem.at[len(handed)])
        copy.start()
        handed.append(copy)

    barrier = pltpu.get_barrier_semaphore()
    for k in range(1, peers):
        pl.semaphore_signal(barrier, inc=1, device_id=(lax.rem(r + k, peers), p), device_id_type=MESH)
    for k in range(1, 4):
        pl.semaphore_signal(barrier, inc=1, device_id=(r, lax.rem(p + k, 4)), device_id_type=MESH)

    for copy in loads[:2]:
        copy.wait()
    forward_list = [toh[0, i] for i in range(blocks)]
    inverse_list = [toz[0, i] for i in range(blocks)]
    srow = slot_of_row([lax.div(b, blocks) for b in forward_list], list(range(blocks)), rows // blocks, rows)
    rrow = slot_of_row([lax.div(b, blocks) for b in inverse_list], inverse_list, rows // blocks, rows)
    slot_ids = lax.broadcasted_iota(jnp.int32, (slot_rows, rows), 0)
    pack = jnp.where(slot_ids == srow, 1.0, 0.0).astype(BF16)
    per_peer = slot_rows // peers
    loads[2].wait()
    out_buf[...] = dot(pack, grad_v[...]).astype(BF16).reshape(peers, per_peer, channels)
    arr_buf[r] = out_buf[r]
    for copy in loads[3:]:
        copy.wait()
    pl.semaphore_wait(barrier, peers - 1 + 3)

    def wave(w, buf):
        across_z, over_x, over_y, over_c = [], [], [], []

        def go(flights, s_sem, r_sem, row, strip, device):
            i = len(flights)
            flights.append((send(buf.at[row, strip], buf.at[row, strip], s_sem.at[w, i], r_sem.at[w, i], device), row))

        def start():
            for k in range(1, zs):
                go(across_z, wz_s, wz_r, r, p, (lax.rem(z + k, zs) * 2 + x, p))
            go(over_x, wx_s, wx_r, r, p, across_x)

        def after_z():
            for k in range(1, zs):
                across_z[k - 1][0].wait_recv()
                row = lax.rem(z + zs - k, zs) * 2 + x
                go(over_x, wx_s, wx_r, row, p, across_x)
                go(over_y, wy_s, wy_r, row, p, across_y)
                go(over_c, wc_s, wc_r, row, p, across_c)

        def after_x():
            for k in range(zs):
                over_x[k][0].wait_recv()
                row = lax.rem(z + zs - k, zs) * 2 + 1 - x
                go(over_y, wy_s, wy_r, row, p, across_y)
                go(over_c, wc_s, wc_r, row, p, across_c)

        def after_y():
            for copy, row in over_y:
                copy.wait_recv()
                go(over_c, wc_s, wc_r, row, p + 2 - 4 * y, across_c)

        def finish():
            for copy, _ in over_c:
                copy.wait_recv()

        return start, after_z, after_x, after_y, finish

    start_q, after_z_q, after_x_q, after_y_q, finish_q = wave(0, wqf)
    start_p, after_z_p, after_x_p, after_y_p, finish_p = wave(1, wpf)
    start_q()
    f_copy = send(fa.at[0], fa.at[1], ff_s, ff_r, across_x)
    after_z_q()
    start_p()
    slot_copies = []
    for k in range(1, peers):
        d = lax.rem(r + k, peers)
        slot_copies.append(send(out_buf.at[d], arr_buf.at[r], sl_s.at[k - 1], sl_r.at[k - 1], (d, p)))
    after_x_q()
    f_copy.wait_recv()
    after_z_p()
    for i in range(2):
        ft[:, i * rows : (i + 1) * rows] = fa[i].astype(F32).T.astype(BF16)
    after_y_q()
    after_x_p()
    finish_q()

    def weight(lo, hi):
        return wqf[:, :, :, lo:hi].reshape(4 * STRIP * peers, hi - lo)

    q_v[...] = dot(fa[0], weight(0, channels)).astype(BF16)
    for i in range(2):
        part = slice(i * rows, (i + 1) * rows)
        k_v[part, :] = dot(fa[i], weight(channels, 2 * channels)).astype(BF16)
        v_v[part, :] = dot(fa[i], weight(2 * channels, 3 * channels)).astype(BF16)

    head_size = channels // HEADS
    scale = head_size ** (-0.5)
    log2e = 1.4426950408889634
    lane = lax.broadcasted_iota(jnp.int32, (1, PAIR), 1)
    masks = [jnp.where(lane < head_size, 1.0, 0.0).astype(BF16), jnp.where(lane < head_size, 0.0, 1.0).astype(BF16)]
    chunks = [reds[9 * i : 9 * i + 9] for i in range(pairs + 1)]
    flights = [{} for _ in chunks]

    def spread(ch, lo, value):
        term = chunks[ch][0]
        value = value.astype(BF16)
        hi = lo + value.shape[1]
        for i in range(4 * peers):
            cc, yy, xx, zz = i % 2, i // 2 % 2, i // 4 % 2, i // 8
            term[cc, yy, xx, zz, :, lo:hi] = value[i * STRIP : (i + 1) * STRIP, :]

    def sem(ch, i):
        return red_s.at[ch, i], red_r.at[ch, i]

    def stage1(ch):
        term, r1 = chunks[ch][0], chunks[ch][1]
        flights[ch][1] = send(term.at[1 - c], r1, *sem(ch, 0), across_c)

    def stage2(ch):
        term, r1, s1, r2 = chunks[ch][:4]
        flights[ch][1].wait_recv()
        s1[...] = (term[c].astype(F32) + r1[...].astype(F32)).astype(BF16)
        flights[ch][2] = send(s1.at[1 - y], r2, *sem(ch, 1), across_y)

    def stage3(ch):
        s1, r2, s2, r3 = chunks[ch][2:6]
        flights[ch][2].wait_recv()
        s2[...] = (s1[y].astype(F32) + r2[...].astype(F32)).astype(BF16)
        flights[ch][3] = send(s2.at[1 - x], r3, *sem(ch, 2), across_x)

    def stage4(ch):
        s2, r3, s3, r4 = chunks[ch][4:8]
        flights[ch][3].wait_recv()
        s3[...] = (s2[x].astype(F32) + r3[...].astype(F32)).astype(BF16)
        flights[ch][4] = []
        for k in range(1, zs):
            zz = lax.rem(z + k, zs)
            flights[ch][4].append(send(s3.at[zz], r4.at[k - 1], *sem(ch, 2 + k), (zz * 2 + x, p)))

    def stage5(ch):
        s3, r4, full = chunks[ch][6:9]
        total = s3[z].astype(F32)
        for k in range(1, zs):
            flights[ch][4][k - 1].wait_recv()
            total = total + r4[k - 1].astype(F32)
        full[p] = total.astype(BF16)
        flights[ch][5] = []
        for k in range(1, 4):
            flights[ch][5].append(send(full.at[p], full.at[p], *sem(ch, 2 + zs - 1 + k), (r, lax.rem(p + k, 4))))

    def stage6(ch):
        full = chunks[ch][8]
        for copy in flights[ch][5]:
            copy.wait_recv()
        value = full[...].astype(F32).reshape(4 * STRIP, full.shape[2])
        if ch > 0:
            for i in range(3):
                lo = i * channels + (ch - 1) * PAIR
                qg_ref[:, lo : lo + PAIR] = value[:, i * PAIR : (i + 1) * PAIR]
        else:
            pg_ref[...] = value
            hand(pg_ref, pg_hbm)

    stages = [stage1, stage2, stage3, stage4, stage5, stage6]

    def tick(t):
        for i, stage in enumerate(stages):
            if 0 <= t - i <= pairs:
                stage(t - i)

    after_y_p()

    def forward(hp, carry):
        cols = pl.ds(pl.multiple_of(hp * PAIR, PAIR), PAIR)
        qp, kp = q_v[:, cols], k_v[:, cols]
        v_t = v_v[:, cols].astype(F32).T.astype(BF16)
        parts = []
        for e in range(2):
            score = contract_cols(kp, qp * masks[e])
            raised = jnp.exp2((score - jnp.max(score, axis=0, keepdims=True)) * (scale * log2e))
            probs = raised * (1.0 / jnp.sum(raised, axis=0, keepdims=True))
            probs_v[2 * hp + e] = probs
            parts.append(dot(v_t[e * head_size : (e + 1) * head_size], probs.astype(BF16)))
        at_v[cols, :] = jnp.concatenate(parts, axis=0).astype(BF16)
        return carry

    lax.fori_loop(0, pairs, forward, 0)
    finish_p()
    for copy in slot_copies:
        copy.wait_recv()
    place = jnp.where(slot_ids == rrow, 1.0, 0.0).astype(BF16)
    h_v[...] = contract_rows(place, arr_buf[...].reshape(slot_rows, channels)).astype(BF16)
    spread(0, 0, dot(at_v[...], h_v[...]))
    tick(0)
    g_v[...] = contract_cols(h_v[...], wpf[...].reshape(4 * STRIP * peers, channels)).astype(BF16)

    terms = []

    def weight_terms(hp):
        dq_b, dk_b, dv_b = terms[hp]
        spread(1 + hp, 0, dot(ft[:, 0:rows], dq_b))
        spread(1 + hp, PAIR, dot(ft[...], dk_b))
        spread(1 + hp, 2 * PAIR, dot(ft[...], dv_b))

    dk_copies = []
    for hp in range(pairs):
        cols = slice(hp * PAIR, (hp + 1) * PAIR)
        qp, kp, vp, gp = q_v[:, cols], k_v[:, cols], v_v[:, cols], g_v[:, cols]
        k_t = kp.astype(F32).T.astype(BF16)
        dk = dv = None
        dq_t = []
        for e in range(2):
            mine = slice(e * head_size, (e + 1) * head_size)
            qm, gm = qp * masks[e], gp * masks[e]
            probs = probs_v[2 * hp + e]
            probs_b = probs.astype(BF16)
            dprob = contract_cols(vp, gm)
            delta = jnp.sum(probs * dprob, axis=0, keepdims=True)
            dscore = (probs * (dprob - delta)).astype(BF16)
            dq_t.append(dot(k_t[mine], dscore))
            dk_e, dv_e = dot(dscore, qm), dot(probs_b, gm)
            dk = dk_e if dk is None else dk + dk_e
            dv = dv_e if dv is None else dv + dv_e
        dq_b = (jnp.concatenate(dq_t, axis=0) * scale).T.astype(BF16)
        dk = dk * scale
        dk_b, dv_b = dk.astype(BF16), dv.astype(BF16)
        dks[hp, 0] = dk_b[rows:]
        dks[hp, 1] = dv_b[rows:]
        dk_copies.append(send(dks.at[hp], dkr.at[hp], dk_s.at[hp], dk_r.at[hp], across_x))
        dq_v[:, cols] = dq_b
        dk_v[:, cols] = dk[:rows]
        dv_v[:, cols] = dv[:rows]
        if hp > 0:
            weight_terms(hp - 1)
            tick(hp)
        terms.append((dq_b, dk_b, dv_b))
    hfeat = contract_cols(dq_v[...], weight(0, channels))
    for lo, hi in ((0, pairs - 1), (pairs - 1, pairs)):
        part = slice(lo * PAIR, hi * PAIR)
        for hp in range(lo, hi):
            cols = slice(hp * PAIR, (hp + 1) * PAIR)
            dk_copies[hp].wait_recv()
            dk_v[:, cols] = dk_v[:, cols] + dkr[hp, 0].astype(F32)
            dv_v[:, cols] = dv_v[:, cols] + dkr[hp, 1].astype(F32)
        hfeat += contract_cols(dk_v[:, part].astype(BF16), weight(channels + lo * PAIR, channels + hi * PAIR))
        hfeat += contract_cols(dv_v[:, part].astype(BF16), weight(2 * channels + lo * PAIR, 2 * channels + hi * PAIR))
    place = jnp.where(slot_ids == rrow, 1.0, 0.0).astype(BF16)
    back_buf[...] = dot(place, hfeat.astype(BF16)).astype(BF16).reshape(peers, per_peer, channels)
    ret_buf[r] = back_buf[r]
    back_copies = []
    for k in range(1, peers):
        d = lax.rem(r + k, peers)
        back_copies.append(send(back_buf.at[d], ret_buf.at[r], bk_s.at[k - 1], bk_r.at[k - 1], (d, p)))
    weight_terms(pairs - 1)
    for t in range(pairs, pairs + 4):
        tick(t)
    for copy in back_copies:
        copy.wait_recv()
    pack = jnp.where(slot_ids == srow, 1.0, 0.0).astype(BF16)
    gf_ref[...] = contract_rows(pack, ret_buf[...].reshape(slot_rows, channels)).astype(BF16)
    hand(gf_ref, gf_hbm)
    for t in range(pairs + 4, pairs + len(stages)):
        tick(t)
    hand(qg_ref, qg_hbm)
    for copy in sends:
        copy.wait_send()
    for copy in handed:
        copy.wait()


def hand_over(*refs):
    count = len(refs) // 2
    copies = [pltpu.make_async_copy(refs[i], refs[count + i], refs[-1].at[i]) for i in range(count)]
    for copy in copies:
        copy.start()
    for copy in copies:
        copy.wait()


def per_device(feats, grad_out, qkv_weight, proj_weight, to_hilbert, to_zorder):
    peers = lax.axis_size("rows")
    feature = feats[0]
    rows, channels = feature.shape
    blocks = to_hilbert.shape[1]
    block = rows // blocks
    slot_rows = peers * CAP * block
    zs = peers // 2
    pairs = channels // PAIR
    share, wide = qkv_weight.shape
    dma = pltpu.SemaphoreType.DMA

    def vm(*shape, kind=BF16):
        return pltpu.VMEM(shape, kind)

    scratch = [
        vm(rows, channels), vm(share, wide, kind=F32), vm(share, channels, kind=F32), dma((3,)),
        vm(peers, 4, STRIP, wide), vm(peers, 4, STRIP, channels),
        dma((2, zs - 1)), dma((2, zs - 1)), dma((2, zs)), dma((2, zs)),
        dma((2, peers - 1)), dma((2, peers - 1)), dma((2, 2 * peers - 2)), dma((2, 2 * peers - 2)),
        vm(peers, slot_rows // peers, channels), vm(peers, slot_rows // peers, channels),
        dma((peers - 1,)), dma((peers - 1,)),
        vm(peers, slot_rows // peers, channels), vm(peers, slot_rows // peers, channels),
        dma((peers - 1,)), dma((peers - 1,)),
        vm(2, rows, channels), vm(channels, 2 * rows), dma, dma,
        vm(rows, channels), vm(2 * rows, channels), vm(2 * rows, channels), vm(rows, channels), vm(rows, channels),
        vm(channels, rows), vm(rows, channels), vm(rows, channels, kind=F32), vm(rows, channels, kind=F32),
        vm(pairs, 2, rows, PAIR), vm(pairs, 2, rows, PAIR), dma((pairs,)), dma((pairs,)),
        dma((pairs + 1, zs + 5)), dma((pairs + 1, zs + 5)),
        vm(rows, channels), pltpu.SMEM((1, blocks), jnp.int32), pltpu.SMEM((1, blocks), jnp.int32), dma((6,)),
        vm(HEADS, 2 * rows, rows, kind=F32),
    ]
    for ch in range(pairs + 1):
        w = 3 * PAIR if ch > 0 else channels
        scratch += [vm(2, 2, 2, zs, STRIP, w), vm(2, 2, zs, STRIP, w), vm(2, 2, zs, STRIP, w),
                    vm(2, zs, STRIP, w), vm(2, zs, STRIP, w), vm(zs, STRIP, w), vm(zs, STRIP, w),
                    vm(zs - 1, STRIP, w), vm(4, STRIP, w)]

    def body(*refs):
        fused_kernel(peers, slot_rows, *refs)

    shapes = (
        jax.ShapeDtypeStruct((rows, channels), BF16),
        jax.ShapeDtypeStruct((share, wide), F32),
        jax.ShapeDtypeStruct((share, channels), F32),
    )
    hbm = pl.BlockSpec(memory_space=pltpu.HBM)
    results = pl.pallas_call(
        body,
        out_shape=shapes,
        in_specs=[hbm] * 6,
        out_specs=(hbm,) * 3,
        scratch_shapes=scratch,
        compiler_params=pltpu.CompilerParams(
            collective_id=0, has_side_effects=True, vmem_limit_bytes=64 * 1024 * 1024
        ),
    )(feature, grad_out[0], qkv_weight.reshape(4, STRIP, -1), proj_weight.reshape(4, STRIP, -1), to_hilbert, to_zorder)
    grad_z, qkv_grad, proj_grad = pl.pallas_call(
        hand_over,
        out_shape=shapes,
        in_specs=[hbm] * 3,
        out_specs=(hbm,) * 3,
        scratch_shapes=[dma((3,))],
        compiler_params=pltpu.CompilerParams(vmem_limit_bytes=64 * 1024 * 1024),
    )(*results)
    return grad_z[None], qkv_grad, proj_grad


def fits_kernel(mesh):
    return mesh.shape["rows"] == 8 and mesh.shape["rep"] == 4


def solution(mesh):
    placed = (
        P("rep", "rows", None),
        P("rep", "rows", None),
        P("rows", None),
        P("rows", None),
        P("rep", "rows"),
        P("rep", "rows"),
    )
    return jax.shard_map(
        per_device if fits_kernel(mesh) else per_device_general,
        mesh=mesh,
        in_specs=placed,
        out_specs=(P("rep", "rows", None), P("rows", None), P("rows", None)),
        check_vma=False,
    )
```

```python
import jax
import jax.numpy as jnp
from jax import lax
from jax.experimental import pallas as pl
from jax.experimental.pallas import tpu as pltpu
from jax.sharding import PartitionSpec as P

HEADS = 8
CAP = 2


def from_partner(block, axis, apart):
    count = lax.axis_size(axis)
    route = []
    for low in range(count):
        high = low | 1 << apart
        if high != low and high < count:
            route += [(low, high), (high, low)]
    return lax.ppermute(block, axis, route)


def move_blocks(outgoing):
    return lax.all_to_all(outgoing, "rows", split_axis=0, concat_axis=0, tiled=True)


def rank_within(order_keys, owners):
    same_owner = owners[None, :] == owners[:, None]
    earlier = order_keys[None, :] < order_keys[:, None]
    return jnp.sum(jnp.logical_and(same_owner, earlier).astype(jnp.int32), axis=1)


def contract_rows(left, right):
    return lax.dot_general(
        left, right, (((0,), (0,)), ((), ())), preferred_element_type=jnp.float32
    )


def contract_cols(left, right):
    return lax.dot_general(
        left, right, (((1,), (1,)), ((), ())), preferred_element_type=jnp.float32
    )


def per_device_general(feats, grad_out, qkv_weight, proj_weight, to_hilbert, to_zorder):
    peer_count = lax.axis_size("rows")
    feature = feats[0]
    rows_dev, channels = feature.shape
    head_size = channels // HEADS
    scale = head_size ** (-0.5)
    blocks_dev = to_hilbert.shape[1]
    slot_count = peer_count * CAP
    w_qkv, w_proj = (
        lax.all_gather(qkv_weight, "rows", axis=0, tiled=True),
        lax.all_gather(proj_weight, "rows", axis=0, tiled=True),
    )
    forward_list = to_hilbert[0]
    inverse_list = to_zorder[0]
    local_ids = jnp.arange(blocks_dev, dtype=jnp.int32)
    slot_ids = jnp.arange(slot_count, dtype=jnp.int32)
    target_dev = forward_list // blocks_dev
    send_slot = target_dev * CAP + rank_within(local_ids, target_dev)
    send_table = (send_slot[None, :] == slot_ids[:, None]).astype(jnp.bfloat16)
    source_dev = inverse_list // blocks_dev
    recv_slot = source_dev * CAP + rank_within(inverse_list, source_dev)
    recv_table = (recv_slot[:, None] == slot_ids[None, :]).astype(jnp.bfloat16)
    zblocks = grad_out[0].reshape(blocks_dev, -1)
    outgoing = jnp.dot(send_table, zblocks, preferred_element_type=jnp.float32).astype(jnp.bfloat16)
    arrived = move_blocks(outgoing.reshape(peer_count, CAP, -1)).reshape(slot_count, -1)
    grad_hil = jnp.dot(recv_table, arrived, preferred_element_type=jnp.float32).astype(jnp.bfloat16)
    grad_hil = grad_hil.reshape(rows_dev, channels)
    qkv = jnp.dot(feature, w_qkv, preferred_element_type=jnp.float32).astype(jnp.bfloat16)
    query = qkv[:, :channels]
    keyval = qkv[:, channels:]
    grad_attn = contract_cols(grad_hil, w_proj).astype(jnp.bfloat16)
    other_kv = from_partner(keyval, "rows", 0)
    keys_all = jnp.concatenate([keyval[:, :channels], other_kv[:, :channels]], axis=0)
    values_all = jnp.concatenate([keyval[:, channels:], other_kv[:, channels:]], axis=0)
    attn_parts, dq_parts, dk_parts, dv_parts = ([], [], [], [])
    for head_index in range(HEADS):
        lo_col = head_index * head_size
        q_head = query[:, lo_col : lo_col + head_size]
        k_head = keys_all[:, lo_col : lo_col + head_size]
        v_head = values_all[:, lo_col : lo_col + head_size]
        g_head = grad_attn[:, lo_col : lo_col + head_size]
        score = contract_cols(q_head, k_head) * scale
        row_max = jnp.max(score, axis=1, keepdims=True)
        raised = jnp.exp(score - row_max)
        row_sum = jnp.sum(raised, axis=1, keepdims=True)
        probs = raised / row_sum
        probs_b = probs.astype(jnp.bfloat16)
        attn_parts.append(
            jnp.dot(probs_b, v_head, preferred_element_type=jnp.float32).astype(jnp.bfloat16)
        )
        dprob = contract_cols(g_head, v_head)
        delta = jnp.sum(probs * dprob, axis=1, keepdims=True)
        dscore = (probs * (dprob - delta) * scale).astype(jnp.bfloat16)
        dq_parts.append(jnp.dot(dscore, k_head, preferred_element_type=jnp.float32))
        dk_parts.append(contract_rows(dscore, q_head))
        dv_parts.append(contract_rows(probs_b, g_head))
    grad_q = jnp.concatenate(dq_parts, axis=1)
    grad_k = jnp.concatenate(dk_parts, axis=1)
    grad_v = jnp.concatenate(dv_parts, axis=1)
    other_k, other_v = (
        from_partner(grad_k[rows_dev:].astype(jnp.bfloat16), "rows", 0).astype(jnp.float32),
        from_partner(grad_v[rows_dev:].astype(jnp.bfloat16), "rows", 0).astype(jnp.float32),
    )
    grad_k = grad_k[:rows_dev] + other_k
    grad_v = grad_v[:rows_dev] + other_v
    grad_qkv = jnp.concatenate([grad_q, grad_k, grad_v], axis=1).astype(jnp.bfloat16)
    attn = jnp.concatenate(attn_parts, axis=1)
    grad_hfeat = contract_cols(grad_qkv, w_qkv).astype(jnp.bfloat16)
    hblocks = grad_hfeat.reshape(blocks_dev, -1)
    going_back = contract_rows(recv_table, hblocks).astype(jnp.bfloat16)
    returned = move_blocks(going_back.reshape(peer_count, CAP, -1)).reshape(slot_count, -1)
    grad_z = contract_rows(send_table, returned).astype(jnp.bfloat16).reshape(rows_dev, channels)
    share = channels // peer_count
    term = jnp.concatenate(
        [contract_rows(feature, grad_qkv), contract_rows(attn, grad_hil)], axis=1
    )
    total = lax.psum(term, ("rows", "rep"))
    owned = lax.dynamic_slice_in_dim(total, lax.axis_index("rows") * share, share, 0)
    return (grad_z[None], owned[:, : 3 * channels], owned[:, 3 * channels :])


MESH = pl.DeviceIdType.MESH
PAIR = 128
STRIP = 16
F32 = jnp.float32
BF16 = jnp.bfloat16


def dot(left, right):
    return jnp.dot(left, right, preferred_element_type=F32)


def slot_of_row(owners, order_keys, block, rows):
    lane = lax.broadcasted_iota(jnp.int32, (1, rows), 1)
    out = lax.rem(lane, block)
    for i, owner in enumerate(owners):
        rank = jnp.int32(0)
        for j, other in enumerate(owners):
            if j != i:
                rank += jnp.where(jnp.logical_and(other == owner, order_keys[j] < order_keys[i]), 1, 0)
        out += jnp.where(lax.div(lane, block) == i, (owner * CAP + rank) * block, 0)
    return out


def fused_kernel(peers, slot_rows, feats_hbm, grad_hbm, wq_hbm, wp_hbm, toh_hbm, toz_hbm,
                 gf_hbm, qg_hbm, pg_hbm,
                 gf_ref, qg_ref, pg_ref, out_sem, wf, wz_s, wz_r, wx_s, wx_r, wy_s, wy_r, wc_s, wc_r,
                 out_buf, arr_buf, sl_s, sl_r, back_buf, ret_buf, bk_s, bk_r,
                 fa, ft, ff_s, ff_r, q_v, k_v, v_v, h_v, at_v, dq_v, dk_v, dv_v, dkb_v, dvb_v, hf_v,
                 dks, dkr, dk_s, dk_r, red_s, red_r, grad_v, toh, toz, in_sem, probs_v,
                 term, r1, s1, r2, s2, r3, s3, r4, full):
    rows, channels = feats_hbm.shape
    blocks = toh_hbm.shape[1]
    wide = wq_hbm.shape[2]
    pairs = channels // PAIR
    shard = 4 * STRIP
    r = lax.axis_index("rows")
    p = lax.axis_index("rep")
    x, z = lax.rem(r, 2), lax.div(r, 2)
    c, y = lax.rem(p, 2), lax.div(p, 2)
    across_x = (r + 1 - 2 * x, p)
    across_c = (r, p + 1 - 2 * c)
    across_y = (r, p + 2 - 4 * y)
    zs = peers // 2

    def remote(src, dst, send_sem, recv_sem, device):
        return pltpu.make_async_remote_copy(
            src_ref=src, dst_ref=dst, send_sem=send_sem, recv_sem=recv_sem,
            device_id=device, device_id_type=MESH)

    def loop(lo, hi, body):
        lax.fori_loop(lo, hi, lambda i, carry: (body(i), carry)[1], 0)

    loads = []
    for i, (src, dst) in enumerate([(toh_hbm, toh), (toz_hbm, toz), (grad_hbm, grad_v),
                                    (wq_hbm, wf.at[r, :, :, pl.ds(0, wide)]),
                                    (wp_hbm, wf.at[r, :, :, pl.ds(wide, channels)]),
                                    (feats_hbm, fa.at[0])]):
        copy = pltpu.make_async_copy(src, dst, in_sem.at[i])
        copy.start()
        loads.append(copy)

    barrier = pltpu.get_barrier_semaphore()

    def greet(device):
        pl.semaphore_signal(barrier, inc=1, device_id=device, device_id_type=MESH)

    loop(1, peers, lambda k: greet((lax.rem(r + k, peers), p)))
    loop(1, 4, lambda k: greet((r, lax.rem(p + k, 4))))

    for copy in loads[:2]:
        copy.wait()
    forward_list = [toh[0, i] for i in range(blocks)]
    inverse_list = [toz[0, i] for i in range(blocks)]
    srow = slot_of_row([lax.div(b, blocks) for b in forward_list], list(range(blocks)), rows // blocks, rows)
    rrow = slot_of_row([lax.div(b, blocks) for b in inverse_list], inverse_list, rows // blocks, rows)
    slot_ids = lax.broadcasted_iota(jnp.int32, (slot_rows, rows), 0)

    def place(row):
        return jnp.where(slot_ids == row, 1.0, 0.0).astype(BF16)

    per_peer = slot_rows // peers
    loads[2].wait()
    out_buf[...] = dot(place(srow), grad_v[...]).astype(BF16).reshape(peers, per_peer, channels)
    arr_buf[r] = out_buf[r]
    for copy in loads[3:]:
        copy.wait()
    pl.semaphore_wait(barrier, peers - 1 + 3)

    def row_of(j):
        return lax.rem(z + zs - lax.rem(j, zs), zs) * 2 + lax.rem(x + lax.div(j, zs), 2)

    def strip_copy(row, strip, s_sem, r_sem, i, device):
        return remote(wf.at[row, strip], wf.at[row, strip], s_sem.at[i], r_sem.at[i], device)

    def by_z(k):
        return strip_copy(r, p, wz_s, wz_r, k - 1, (lax.rem(z + k, zs) * 2 + x, p))

    def by_x(k):
        return strip_copy(row_of(k), p, wx_s, wx_r, k, across_x)

    def by_y(j):
        return strip_copy(row_of(j), p, wy_s, wy_r, j - 1, across_y)

    def by_c(j):
        return strip_copy(row_of(j), p, wc_s, wc_r, j - 1, across_c)

    def by_yc(j):
        return strip_copy(row_of(j), p + 2 - 4 * y, wc_s, wc_r, peers - 2 + j, across_c)

    def slot_copy(k):
        d = lax.rem(r + k, peers)
        return remote(out_buf.at[d], arr_buf.at[r], sl_s.at[k - 1], sl_r.at[k - 1], (d, p))

    def back_copy(k):
        d = lax.rem(r + k, peers)
        return remote(back_buf.at[d], ret_buf.at[r], bk_s.at[k - 1], bk_r.at[k - 1], (d, p))

    feats_copy = remote(fa.at[0], fa.at[1], ff_s, ff_r, across_x)

    loop(1, zs, lambda k: by_z(k).start())
    by_x(0).start()
    feats_copy.start()

    def after_z(k):
        by_z(k).wait_recv()
        by_x(k).start()
        by_y(k).start()
        by_c(k).start()

    def after_x(k):
        by_x(k).wait_recv()
        by_y(zs + k).start()
        by_c(zs + k).start()

    def after_y(j):
        by_y(j).wait_recv()
        by_yc(j).start()

    def after_c(j):
        by_c(j).wait_recv()
        by_yc(j).wait_recv()

    loop(1, zs, after_z)
    loop(1, peers, lambda k: slot_copy(k).start())
    loop(0, zs, after_x)
    feats_copy.wait_recv()

    def turn(i):
        ft[:, pl.ds(pl.multiple_of(i * rows, rows), rows)] = fa[i].astype(F32).T.astype(BF16)

    loop(0, 2, turn)
    loop(1, peers, after_y)
    loop(1, peers, after_c)

    def pair_cols(hp, base=0):
        return pl.ds(pl.multiple_of(base + hp * PAIR, PAIR), PAIR)

    def weight(i, hp):
        return wf[:, :, :, pair_cols(hp, i * channels)].reshape(shard * peers, PAIR)

    head_size = channels // HEADS
    scale = head_size ** (-0.5)
    log2e = 1.4426950408889634
    lane = lax.broadcasted_iota(jnp.int32, (1, PAIR), 1)
    masks = [jnp.where(lane < head_size, 1.0, 0.0).astype(BF16), jnp.where(lane < head_size, 0.0, 1.0).astype(BF16)]

    def forward(hp):
        cols = pair_cols(hp)
        both = fa[...].reshape(2 * rows, channels)
        qp = dot(fa[0], weight(0, hp)).astype(BF16)
        kp = dot(both, weight(1, hp)).astype(BF16)
        vp = dot(both, weight(2, hp)).astype(BF16)
        q_v[:, cols], k_v[:, cols], v_v[:, cols] = qp, kp, vp
        v_t = vp.astype(F32).T.astype(BF16)
        parts = []
        for e in range(2):
            score = contract_cols(kp, qp * masks[e])
            raised = jnp.exp2((score - jnp.max(score, axis=0, keepdims=True)) * (scale * log2e))
            probs = raised * (1.0 / jnp.sum(raised, axis=0, keepdims=True))
            probs_v[2 * hp + e] = probs
            parts.append(dot(v_t[e * head_size : (e + 1) * head_size], probs.astype(BF16)))
        at_v[cols, :] = jnp.concatenate(parts, axis=0).astype(BF16)

    loop(0, pairs, forward)
    loop(1, peers, lambda k: slot_copy(k).wait_recv())
    h_v[...] = contract_rows(place(rrow), arr_buf[...].reshape(slot_rows, channels)).astype(BF16)
    hf_v[...] = jnp.zeros_like(hf_v)

    def dk_copy(hp):
        return remote(dks.at[hp], dkr.at[hp], dk_s.at[hp], dk_r.at[hp], across_x)

    def backward(hp):
        cols = pair_cols(hp)
        qp, kp, vp = q_v[:, cols], k_v[:, cols], v_v[:, cols]
        w_rows = wf[pl.ds(hp * (PAIR // shard), PAIR // shard), :, :, wide:].reshape(PAIR, channels)
        gp = contract_cols(h_v[...], w_rows).astype(BF16)
        k_t = kp.astype(F32).T.astype(BF16)
        dk = dv = None
        dq_t = []
        for e in range(2):
            mine = slice(e * head_size, (e + 1) * head_size)
            qm, gm = qp * masks[e], gp * masks[e]
            probs = probs_v[2 * hp + e]
            probs_b = probs.astype(BF16)
            dprob = contract_cols(vp, gm)
            delta = jnp.sum(probs * dprob, axis=0, keepdims=True)
            dscore = (probs * (dprob - delta)).astype(BF16)
            dq_t.append(dot(k_t[mine], dscore))
            dk_e, dv_e = dot(dscore, qm), dot(probs_b, gm)
            dk = dk_e if dk is None else dk + dk_e
            dv = dv_e if dv is None else dv + dv_e
        dk = dk * scale
        dk_b, dv_b = dk.astype(BF16), dv.astype(BF16)
        dks[hp, 0] = dk_b[rows:]
        dks[hp, 1] = dv_b[rows:]
        dk_copy(hp).start()
        dq_v[:, cols] = (jnp.concatenate(dq_t, axis=0) * scale).T.astype(BF16)
        dk_v[:, cols], dv_v[:, cols] = dk[:rows], dv[:rows]
        dkb_v[:, cols], dvb_v[:, cols] = dk_b, dv_b

    def add_hfeat(hp):
        cols = pair_cols(hp)
        dk_copy(hp).wait_recv()
        dk = (dk_v[:, cols] + dkr[hp, 0].astype(F32)).astype(BF16)
        dv = (dv_v[:, cols] + dkr[hp, 1].astype(F32)).astype(BF16)
        left = jnp.concatenate([dq_v[:, cols], dk, dv], axis=1)
        right = jnp.concatenate([weight(i, hp) for i in range(3)], axis=1)
        hf_v[...] += contract_cols(left, right)

    def go_back():
        back_buf[...] = dot(place(rrow), hf_v[...].astype(BF16)).astype(BF16).reshape(peers, per_peer, channels)
        ret_buf[r] = back_buf[r]
        loop(1, peers, lambda k: back_copy(k).start())

    def red(ch, i, src, dst, device):
        return remote(src, dst, red_s.at[ch, i], red_r.at[ch, i], device)

    def red1(ch):
        return red(ch, 0, term.at[ch, 1 - c], r1.at[ch], across_c)

    def red2(ch):
        return red(ch, 1, s1.at[ch, 1 - y], r2.at[ch], across_y)

    def red3(ch):
        return red(ch, 2, s2.at[ch, 1 - x], r3.at[ch], across_x)

    def red4(ch, k):
        zz = lax.rem(z + k, zs)
        return red(ch, 2 + k, s3.at[ch, zz], r4.at[ch, k - 1], (zz * 2 + x, p))

    def red5(ch, k):
        return red(ch, 1 + zs + k, full.at[ch, p], full.at[ch, p], (r, lax.rem(p + k, 4)))

    def stage1(ch):
        cols = pair_cols(ch)
        parts = [dot(ft[:, 0:rows], dq_v[:, cols]), dot(ft[...], dkb_v[:, cols]), dot(ft[...], dvb_v[:, cols]),
                 dot(at_v[...], h_v[:, cols])]
        for j, part in enumerate(parts):
            part = part.astype(BF16)
            for i in range(4 * peers):
                cc, yy, xx, zz = i % 2, i // 2 % 2, i // 4 % 2, i // 8
                term[ch, cc, yy, xx, zz, :, j * PAIR : (j + 1) * PAIR] = part[i * STRIP : (i + 1) * STRIP, :]
        red1(ch).start()

    def stage2(ch):
        red1(ch).wait_recv()
        s1[ch] = (term[ch, c].astype(F32) + r1[ch].astype(F32)).astype(BF16)
        red2(ch).start()

    def stage3(ch):
        red2(ch).wait_recv()
        s2[ch] = (s1[ch, y].astype(F32) + r2[ch].astype(F32)).astype(BF16)
        red3(ch).start()

    def stage4(ch):
        red3(ch).wait_recv()
        s3[ch] = (s2[ch, x].astype(F32) + r3[ch].astype(F32)).astype(BF16)
        for k in range(1, zs):
            red4(ch, k).start()

    def stage5(ch):
        total = s3[ch, z].astype(F32)
        for k in range(1, zs):
            red4(ch, k).wait_recv()
            total = total + r4[ch, k - 1].astype(F32)
        full[ch, p] = total.astype(BF16)
        for k in range(1, 4):
            red5(ch, k).start()

    def stage6(ch):
        for k in range(1, 4):
            red5(ch, k).wait_recv()
        value = full[ch].astype(F32).reshape(shard, 4 * PAIR)
        for i in range(3):
            qg_ref[:, pair_cols(ch, i * channels)] = value[:, i * PAIR : (i + 1) * PAIR]
        pg_ref[:, pair_cols(ch)] = value[:, 3 * PAIR :]

    stages = [stage1, stage2, stage3, stage4, stage5, stage6]

    def tick(t):
        pl.when(t < pairs)(lambda: backward(t))
        pl.when(jnp.logical_and(t >= 1, t <= pairs))(lambda: add_hfeat(t - 1))
        pl.when(t == pairs)(go_back)
        for i, stage in enumerate(stages):
            pl.when(jnp.logical_and(t >= i + 1, t < i + 1 + pairs))(lambda stage=stage, i=i: stage(t - i - 1))

    loop(0, pairs + len(stages), tick)
    outs = [pltpu.make_async_copy(src, dst, out_sem.at[i])
            for i, (src, dst) in enumerate([(qg_ref, qg_hbm), (pg_ref, pg_hbm), (gf_ref, gf_hbm)])]
    outs[0].start()
    outs[1].start()
    loop(1, peers, lambda k: back_copy(k).wait_recv())
    gf_ref[...] = contract_rows(place(srow), ret_buf[...].reshape(slot_rows, channels)).astype(BF16)
    outs[2].start()

    def sent_rows(k):
        slot_copy(k).wait_send()
        back_copy(k).wait_send()
        by_y(k).wait_send()
        by_c(k).wait_send()
        by_yc(k).wait_send()

    def sent_chunk(ch):
        dk_copy(ch).wait_send()
        for one in (red1, red2, red3):
            one(ch).wait_send()
        for k in range(1, zs):
            red4(ch, k).wait_send()
        for k in range(1, 4):
            red5(ch, k).wait_send()

    loop(1, zs, lambda k: by_z(k).wait_send())
    loop(0, zs, lambda k: by_x(k).wait_send())
    feats_copy.wait_send()
    loop(1, peers, sent_rows)
    loop(0, pairs, sent_chunk)
    for copy in outs:
        copy.wait()


def hand_over(*refs):
    count = (len(refs) - 2) // 3
    ins, outs, held = refs[:count], refs[count : 2 * count], refs[2 * count : 3 * count]
    first = [pltpu.make_async_copy(ins[i], held[i], refs[-2].at[i]) for i in range(count)]
    second = [pltpu.make_async_copy(held[i], outs[i], refs[-1].at[i]) for i in range(count)]
    for copy in first:
        copy.start()
    for i in range(count):
        first[i].wait()
        second[i].start()
    for copy in second:
        copy.wait()


def per_device(feats, grad_out, qkv_weight, proj_weight, to_hilbert, to_zorder):
    peers = lax.axis_size("rows")
    feature = feats[0]
    rows, channels = feature.shape
    blocks = to_hilbert.shape[1]
    block = rows // blocks
    slot_rows = peers * CAP * block
    zs = peers // 2
    pairs = channels // PAIR
    share, wide = qkv_weight.shape
    dma = pltpu.SemaphoreType.DMA

    def vm(*shape, kind=BF16):
        return pltpu.VMEM(shape, kind)

    width = 4 * PAIR
    scratch = [
        vm(rows, channels), vm(share, wide, kind=F32), vm(share, channels, kind=F32), dma((3,)),
        vm(peers, 4, STRIP, wide + channels),
        dma((zs - 1,)), dma((zs - 1,)), dma((zs,)), dma((zs,)),
        dma((peers - 1,)), dma((peers - 1,)), dma((2 * peers - 2,)), dma((2 * peers - 2,)),
        vm(peers, slot_rows // peers, channels), vm(peers, slot_rows // peers, channels),
        dma((peers - 1,)), dma((peers - 1,)),
        vm(peers, slot_rows // peers, channels), vm(peers, slot_rows // peers, channels),
        dma((peers - 1,)), dma((peers - 1,)),
        vm(2, rows, channels), vm(channels, 2 * rows), dma, dma,
        vm(rows, channels), vm(2 * rows, channels), vm(2 * rows, channels), vm(rows, channels),
        vm(channels, rows), vm(rows, channels), vm(rows, channels, kind=F32), vm(rows, channels, kind=F32),
        vm(2 * rows, channels), vm(2 * rows, channels), vm(rows, channels, kind=F32),
        vm(pairs, 2, rows, PAIR), vm(pairs, 2, rows, PAIR), dma((pairs,)), dma((pairs,)),
        dma((pairs, zs + 5)), dma((pairs, zs + 5)),
        vm(rows, channels), pltpu.SMEM((1, blocks), jnp.int32), pltpu.SMEM((1, blocks), jnp.int32), dma((6,)),
        vm(HEADS, 2 * rows, rows, kind=F32),
        vm(pairs, 2, 2, 2, zs, STRIP, width), vm(pairs, 2, 2, zs, STRIP, width), vm(pairs, 2, 2, zs, STRIP, width),
        vm(pairs, 2, zs, STRIP, width), vm(pairs, 2, zs, STRIP, width),
        vm(pairs, zs, STRIP, width), vm(pairs, zs, STRIP, width),
        vm(pairs, zs - 1, STRIP, width), vm(pairs, 4, STRIP, width),
    ]

    def body(*refs):
        fused_kernel(peers, slot_rows, *refs)

    shapes = (
        jax.ShapeDtypeStruct((rows, channels), BF16),
        jax.ShapeDtypeStruct((share, wide), F32),
        jax.ShapeDtypeStruct((share, channels), F32),
    )
    hbm = pl.BlockSpec(memory_space=pltpu.HBM)
    results = pl.pallas_call(
        body,
        out_shape=shapes,
        in_specs=[hbm] * 6,
        out_specs=(hbm,) * 3,
        scratch_shapes=scratch,
        compiler_params=pltpu.CompilerParams(
            collective_id=0, has_side_effects=True, vmem_limit_bytes=64 * 1024 * 1024
        ),
    )(feature, grad_out[0], qkv_weight.reshape(4, STRIP, -1), proj_weight.reshape(4, STRIP, -1), to_hilbert, to_zorder)
    grad_z, qkv_grad, proj_grad = pl.pallas_call(
        hand_over,
        out_shape=shapes,
        in_specs=[hbm] * 3,
        out_specs=(hbm,) * 3,
        scratch_shapes=[pltpu.VMEM(one.shape, one.dtype) for one in shapes] + [dma((3,)), dma((3,))],
        compiler_params=pltpu.CompilerParams(vmem_limit_bytes=64 * 1024 * 1024),
    )(*results)
    return grad_z[None], qkv_grad, proj_grad


def fits_kernel(mesh):
    return mesh.shape["rows"] == 8 and mesh.shape["rep"] == 4


def solution(mesh):
    placed = (
        P("rep", "rows", None),
        P("rep", "rows", None),
        P("rows", None),
        P("rows", None),
        P("rep", "rows"),
        P("rep", "rows"),
    )
    return jax.shard_map(
        per_device if fits_kernel(mesh) else per_device_general,
        mesh=mesh,
        in_specs=placed,
        out_specs=(P("rep", "rows", None), P("rows", None), P("rows", None)),
        check_vma=False,
    )
```

```python
import jax
import jax.numpy as jnp
from jax import lax
from jax.experimental import pallas as pl
from jax.experimental.pallas import tpu as pltpu
from jax.sharding import PartitionSpec as P

HEADS = 8
CAP = 2


def from_partner(block, axis, apart):
    count = lax.axis_size(axis)
    route = []
    for low in range(count):
        high = low | 1 << apart
        if high != low and high < count:
            route += [(low, high), (high, low)]
    return lax.ppermute(block, axis, route)


def move_blocks(outgoing):
    return lax.all_to_all(outgoing, "rows", split_axis=0, concat_axis=0, tiled=True)


def rank_within(order_keys, owners):
    same_owner = owners[None, :] == owners[:, None]
    earlier = order_keys[None, :] < order_keys[:, None]
    return jnp.sum(jnp.logical_and(same_owner, earlier).astype(jnp.int32), axis=1)


def contract_rows(left, right):
    return lax.dot_general(
        left, right, (((0,), (0,)), ((), ())), preferred_element_type=jnp.float32
    )


def contract_cols(left, right):
    return lax.dot_general(
        left, right, (((1,), (1,)), ((), ())), preferred_element_type=jnp.float32
    )


def per_device_general(feats, grad_out, qkv_weight, proj_weight, to_hilbert, to_zorder):
    peer_count = lax.axis_size("rows")
    feature = feats[0]
    rows_dev, channels = feature.shape
    head_size = channels // HEADS
    scale = head_size ** (-0.5)
    blocks_dev = to_hilbert.shape[1]
    slot_count = peer_count * CAP
    w_qkv, w_proj = (
        lax.all_gather(qkv_weight, "rows", axis=0, tiled=True),
        lax.all_gather(proj_weight, "rows", axis=0, tiled=True),
    )
    forward_list = to_hilbert[0]
    inverse_list = to_zorder[0]
    local_ids = jnp.arange(blocks_dev, dtype=jnp.int32)
    slot_ids = jnp.arange(slot_count, dtype=jnp.int32)
    target_dev = forward_list // blocks_dev
    send_slot = target_dev * CAP + rank_within(local_ids, target_dev)
    send_table = (send_slot[None, :] == slot_ids[:, None]).astype(jnp.bfloat16)
    source_dev = inverse_list // blocks_dev
    recv_slot = source_dev * CAP + rank_within(inverse_list, source_dev)
    recv_table = (recv_slot[:, None] == slot_ids[None, :]).astype(jnp.bfloat16)
    zblocks = grad_out[0].reshape(blocks_dev, -1)
    outgoing = jnp.dot(send_table, zblocks, preferred_element_type=jnp.float32).astype(jnp.bfloat16)
    arrived = move_blocks(outgoing.reshape(peer_count, CAP, -1)).reshape(slot_count, -1)
    grad_hil = jnp.dot(recv_table, arrived, preferred_element_type=jnp.float32).astype(jnp.bfloat16)
    grad_hil = grad_hil.reshape(rows_dev, channels)
    qkv = jnp.dot(feature, w_qkv, preferred_element_type=jnp.float32).astype(jnp.bfloat16)
    query = qkv[:, :channels]
    keyval = qkv[:, channels:]
    grad_attn = contract_cols(grad_hil, w_proj).astype(jnp.bfloat16)
    other_kv = from_partner(keyval, "rows", 0)
    keys_all = jnp.concatenate([keyval[:, :channels], other_kv[:, :channels]], axis=0)
    values_all = jnp.concatenate([keyval[:, channels:], other_kv[:, channels:]], axis=0)
    attn_parts, dq_parts, dk_parts, dv_parts = ([], [], [], [])
    for head_index in range(HEADS):
        lo_col = head_index * head_size
        q_head = query[:, lo_col : lo_col + head_size]
        k_head = keys_all[:, lo_col : lo_col + head_size]
        v_head = values_all[:, lo_col : lo_col + head_size]
        g_head = grad_attn[:, lo_col : lo_col + head_size]
        score = contract_cols(q_head, k_head) * scale
        row_max = jnp.max(score, axis=1, keepdims=True)
        raised = jnp.exp(score - row_max)
        row_sum = jnp.sum(raised, axis=1, keepdims=True)
        probs = raised / row_sum
        probs_b = probs.astype(jnp.bfloat16)
        attn_parts.append(
            jnp.dot(probs_b, v_head, preferred_element_type=jnp.float32).astype(jnp.bfloat16)
        )
        dprob = contract_cols(g_head, v_head)
        delta = jnp.sum(probs * dprob, axis=1, keepdims=True)
        dscore = (probs * (dprob - delta) * scale).astype(jnp.bfloat16)
        dq_parts.append(jnp.dot(dscore, k_head, preferred_element_type=jnp.float32))
        dk_parts.append(contract_rows(dscore, q_head))
        dv_parts.append(contract_rows(probs_b, g_head))
    grad_q = jnp.concatenate(dq_parts, axis=1)
    grad_k = jnp.concatenate(dk_parts, axis=1)
    grad_v = jnp.concatenate(dv_parts, axis=1)
    other_k, other_v = (
        from_partner(grad_k[rows_dev:].astype(jnp.bfloat16), "rows", 0).astype(jnp.float32),
        from_partner(grad_v[rows_dev:].astype(jnp.bfloat16), "rows", 0).astype(jnp.float32),
    )
    grad_k = grad_k[:rows_dev] + other_k
    grad_v = grad_v[:rows_dev] + other_v
    grad_qkv = jnp.concatenate([grad_q, grad_k, grad_v], axis=1).astype(jnp.bfloat16)
    attn = jnp.concatenate(attn_parts, axis=1)
    grad_hfeat = contract_cols(grad_qkv, w_qkv).astype(jnp.bfloat16)
    hblocks = grad_hfeat.reshape(blocks_dev, -1)
    going_back = contract_rows(recv_table, hblocks).astype(jnp.bfloat16)
    returned = move_blocks(going_back.reshape(peer_count, CAP, -1)).reshape(slot_count, -1)
    grad_z = contract_rows(send_table, returned).astype(jnp.bfloat16).reshape(rows_dev, channels)
    share = channels // peer_count
    term = jnp.concatenate(
        [contract_rows(feature, grad_qkv), contract_rows(attn, grad_hil)], axis=1
    )
    total = lax.psum(term, ("rows", "rep"))
    owned = lax.dynamic_slice_in_dim(total, lax.axis_index("rows") * share, share, 0)
    return (grad_z[None], owned[:, : 3 * channels], owned[:, 3 * channels :])


MESH = pl.DeviceIdType.MESH
PAIR = 128
STRIP = 16
F32 = jnp.float32
BF16 = jnp.bfloat16


def dot(left, right):
    return jnp.dot(left, right, preferred_element_type=F32)


def slot_of_row(owners, order_keys, block, rows):
    lane = lax.broadcasted_iota(jnp.int32, (1, rows), 1)
    out = lax.rem(lane, block)
    for i, owner in enumerate(owners):
        rank = jnp.int32(0)
        for j, other in enumerate(owners):
            if j != i:
                rank += jnp.where(jnp.logical_and(other == owner, order_keys[j] < order_keys[i]), 1, 0)
        out += jnp.where(lax.div(lane, block) == i, (owner * CAP + rank) * block, 0)
    return out


def fused_kernel(peers, slot_rows, feats_hbm, grad_hbm, wq_hbm, wp_hbm, toh_hbm, toz_hbm,
                 gf_hbm, qg_hbm, pg_hbm,
                 gf_ref, qg_ref, pg_ref, out_sem, wf, wz_s, wz_r, wx_s, wx_r, wy_s, wy_r, wc_s, wc_r,
                 out_buf, arr_buf, sl_s, sl_r, back_buf, ret_buf, bk_s, bk_r,
                 fa, ft, ff_s, ff_r, q_v, k_v, v_v, h_v, at_v, dq_v, dk_v, dv_v, dkb_v, dvb_v, hf_v,
                 dks, dkr, dk_s, dk_r, red_s, red_r, grad_v, toh, toz, in_sem, probs_v,
                 term, r1, s1, r2, s2, r3, s3, r4, full):
    rows, channels = feats_hbm.shape
    blocks = toh_hbm.shape[1]
    wide = wq_hbm.shape[2]
    pairs = channels // PAIR
    shard = 4 * STRIP
    r = lax.axis_index("rows")
    p = lax.axis_index("rep")
    x, z = lax.rem(r, 2), lax.div(r, 2)
    c, y = lax.rem(p, 2), lax.div(p, 2)
    across_x = (r + 1 - 2 * x, p)
    across_c = (r, p + 1 - 2 * c)
    across_y = (r, p + 2 - 4 * y)
    zs = peers // 2

    def remote(src, dst, send_sem, recv_sem, device):
        return pltpu.make_async_remote_copy(
            src_ref=src, dst_ref=dst, send_sem=send_sem, recv_sem=recv_sem,
            device_id=device, device_id_type=MESH)

    def loop(lo, hi, body):
        lax.fori_loop(lo, hi, lambda i, carry: (body(i), carry)[1], 0)

    loads = []
    for i, (src, dst) in enumerate([(toh_hbm, toh), (toz_hbm, toz), (grad_hbm, grad_v),
                                    (wq_hbm, wf.at[r, :, :, pl.ds(0, wide)]),
                                    (wp_hbm, wf.at[r, :, :, pl.ds(wide, channels)]),
                                    (feats_hbm, fa.at[0])]):
        copy = pltpu.make_async_copy(src, dst, in_sem.at[i])
        copy.start()
        loads.append(copy)

    barrier = pltpu.get_barrier_semaphore()

    def greet(device):
        pl.semaphore_signal(barrier, inc=1, device_id=device, device_id_type=MESH)

    loop(1, peers, lambda k: greet((lax.rem(r + k, peers), p)))
    loop(1, 4, lambda k: greet((r, lax.rem(p + k, 4))))


    def place(row):
        return jnp.where(slot_ids == row, 1.0, 0.0).astype(BF16)

    per_peer = slot_rows // peers
    for copy in loads[3:5]:
        copy.wait()
    pl.semaphore_wait(barrier, peers - 1 + 3)

    def row_of(j):
        return lax.rem(z + zs - lax.rem(j, zs), zs) * 2 + lax.rem(x + lax.div(j, zs), 2)

    def strip_copy(row, strip, s_sem, r_sem, i, device):
        return remote(wf.at[row, strip], wf.at[row, strip], s_sem.at[i], r_sem.at[i], device)

    def by_z(k):
        return strip_copy(r, p, wz_s, wz_r, k - 1, (lax.rem(z + k, zs) * 2 + x, p))

    def by_x(k):
        return strip_copy(row_of(k), p, wx_s, wx_r, k, across_x)

    def by_y(j):
        return strip_copy(row_of(j), p, wy_s, wy_r, j - 1, across_y)

    def by_c(j):
        return strip_copy(row_of(j), p, wc_s, wc_r, j - 1, across_c)

    def by_yc(j):
        return strip_copy(row_of(j), p + 2 - 4 * y, wc_s, wc_r, peers - 2 + j, across_c)

    def slot_copy(k):
        d = lax.rem(r + k, peers)
        return remote(out_buf.at[d], arr_buf.at[r], sl_s.at[k - 1], sl_r.at[k - 1], (d, p))

    def back_copy(k):
        d = lax.rem(r + k, peers)
        return remote(back_buf.at[d], ret_buf.at[r], bk_s.at[k - 1], bk_r.at[k - 1], (d, p))

    feats_copy = remote(fa.at[0], fa.at[1], ff_s, ff_r, across_x)

    loop(1, zs, lambda k: by_z(k).start())
    by_x(0).start()
    for copy in loads[:2]:
        copy.wait()
    forward_list = [toh[0, i] for i in range(blocks)]
    inverse_list = [toz[0, i] for i in range(blocks)]
    srow = slot_of_row([lax.div(b, blocks) for b in forward_list], list(range(blocks)), rows // blocks, rows)
    rrow = slot_of_row([lax.div(b, blocks) for b in inverse_list], inverse_list, rows // blocks, rows)
    slot_ids = lax.broadcasted_iota(jnp.int32, (slot_rows, rows), 0)
    loads[2].wait()
    out_buf[...] = dot(place(srow), grad_v[...]).astype(BF16).reshape(peers, per_peer, channels)
    arr_buf[r] = out_buf[r]

    def after_z(k):
        by_z(k).wait_recv()
        by_x(k).start()
        by_y(k).start()
        by_c(k).start()

    def after_x(k):
        by_x(k).wait_recv()
        by_y(zs + k).start()
        by_c(zs + k).start()

    def after_y(j):
        by_y(j).wait_recv()
        by_yc(j).start()

    def after_c(j):
        by_c(j).wait_recv()
        by_yc(j).wait_recv()

    loop(1, zs, after_z)
    loads[5].wait()
    feats_copy.start()
    loop(0, zs, after_x)
    loop(1, peers, lambda k: slot_copy(k).start())
    feats_copy.wait_recv()

    def turn(i):
        ft[:, pl.ds(pl.multiple_of(i * rows, rows), rows)] = fa[i].astype(F32).T.astype(BF16)

    loop(0, 2, turn)
    loop(1, peers, after_y)
    loop(1, peers, after_c)

    def pair_cols(hp, base=0):
        return pl.ds(pl.multiple_of(base + hp * PAIR, PAIR), PAIR)

    def weight(i, hp):
        return wf[:, :, :, pair_cols(hp, i * channels)].reshape(shard * peers, PAIR)

    head_size = channels // HEADS
    scale = head_size ** (-0.5)
    log2e = 1.4426950408889634
    lane = lax.broadcasted_iota(jnp.int32, (1, PAIR), 1)
    masks = [jnp.where(lane < head_size, 1.0, 0.0).astype(BF16), jnp.where(lane < head_size, 0.0, 1.0).astype(BF16)]

    def forward(hp):
        cols = pair_cols(hp)
        both = fa[...].reshape(2 * rows, channels)
        qp = dot(fa[0], weight(0, hp)).astype(BF16)
        kp = dot(both, weight(1, hp)).astype(BF16)
        vp = dot(both, weight(2, hp)).astype(BF16)
        q_v[:, cols], k_v[:, cols], v_v[:, cols] = qp, kp, vp
        v_t = vp.astype(F32).T.astype(BF16)
        parts = []
        for e in range(2):
            score = contract_cols(kp, qp * masks[e])
            raised = jnp.exp2((score - jnp.max(score, axis=0, keepdims=True)) * (scale * log2e))
            probs = raised * (1.0 / jnp.sum(raised, axis=0, keepdims=True))
            probs_v[2 * hp + e] = probs
            parts.append(dot(v_t[e * head_size : (e + 1) * head_size], probs.astype(BF16)))
        at_v[cols, :] = jnp.concatenate(parts, axis=0).astype(BF16)

    loop(0, pairs, forward)
    loop(1, peers, lambda k: slot_copy(k).wait_recv())
    h_v[...] = contract_rows(place(rrow), arr_buf[...].reshape(slot_rows, channels)).astype(BF16)
    hf_v[...] = jnp.zeros_like(hf_v)

    def dk_copy(hp):
        return remote(dks.at[hp], dkr.at[hp], dk_s.at[hp], dk_r.at[hp], across_x)

    def backward(hp):
        cols = pair_cols(hp)
        qp, kp, vp = q_v[:, cols], k_v[:, cols], v_v[:, cols]
        w_rows = wf[pl.ds(hp * (PAIR // shard), PAIR // shard), :, :, wide:].reshape(PAIR, channels)
        gp = contract_cols(h_v[...], w_rows).astype(BF16)
        k_t = kp.astype(F32).T.astype(BF16)
        dk = dv = None
        dq_t = []
        for e in range(2):
            mine = slice(e * head_size, (e + 1) * head_size)
            qm, gm = qp * masks[e], gp * masks[e]
            probs = probs_v[2 * hp + e]
            probs_b = probs.astype(BF16)
            dprob = contract_cols(vp, gm)
            delta = jnp.sum(probs * dprob, axis=0, keepdims=True)
            dscore = (probs * (dprob - delta)).astype(BF16)
            dq_t.append(dot(k_t[mine], dscore))
            dk_e, dv_e = dot(dscore, qm), dot(probs_b, gm)
            dk = dk_e if dk is None else dk + dk_e
            dv = dv_e if dv is None else dv + dv_e
        dk = dk * scale
        dk_b, dv_b = dk.astype(BF16), dv.astype(BF16)
        dks[hp, 0] = dk_b[rows:]
        dks[hp, 1] = dv_b[rows:]
        dk_copy(hp).start()
        dq_v[:, cols] = (jnp.concatenate(dq_t, axis=0) * scale).T.astype(BF16)
        dk_v[:, cols], dv_v[:, cols] = dk[:rows], dv[:rows]
        dkb_v[:, cols], dvb_v[:, cols] = dk_b, dv_b

    def add_hfeat(hp):
        cols = pair_cols(hp)
        dk_copy(hp).wait_recv()
        dk = (dk_v[:, cols] + dkr[hp, 0].astype(F32)).astype(BF16)
        dv = (dv_v[:, cols] + dkr[hp, 1].astype(F32)).astype(BF16)
        left = jnp.concatenate([dq_v[:, cols], dk, dv], axis=1)
        right = jnp.concatenate([weight(i, hp) for i in range(3)], axis=1)
        hf_v[...] += contract_cols(left, right)

    def go_back():
        back_buf[...] = dot(place(rrow), hf_v[...].astype(BF16)).astype(BF16).reshape(peers, per_peer, channels)
        ret_buf[r] = back_buf[r]
        loop(1, peers, lambda k: back_copy(k).start())

    def red(ch, i, src, dst, device):
        return remote(src, dst, red_s.at[ch, i], red_r.at[ch, i], device)

    def red1(ch):
        return red(ch, 0, term.at[ch, 1 - c], r1.at[ch], across_c)

    def red2(ch):
        return red(ch, 1, s1.at[ch, 1 - y], r2.at[ch], across_y)

    def red3(ch):
        return red(ch, 2, s2.at[ch, 1 - x], r3.at[ch], across_x)

    def red4(ch, k):
        zz = lax.rem(z + k, zs)
        return red(ch, 2 + k, s3.at[ch, zz], r4.at[ch, k - 1], (zz * 2 + x, p))

    def red5(ch, k):
        return red(ch, 1 + zs + k, full.at[ch, p], full.at[ch, p], (r, lax.rem(p + k, 4)))

    def stage1(ch):
        cols = pair_cols(ch)
        parts = [dot(ft[:, 0:rows], dq_v[:, cols]), dot(ft[...], dkb_v[:, cols]), dot(ft[...], dvb_v[:, cols]),
                 dot(at_v[...], h_v[:, cols])]
        for j, part in enumerate(parts):
            part = part.astype(BF16)
            for i in range(4 * peers):
                cc, yy, xx, zz = i % 2, i // 2 % 2, i // 4 % 2, i // 8
                term[ch, cc, yy, xx, zz, :, j * PAIR : (j + 1) * PAIR] = part[i * STRIP : (i + 1) * STRIP, :]
        red1(ch).start()

    def stage2(ch):
        red1(ch).wait_recv()
        s1[ch] = (term[ch, c].astype(F32) + r1[ch].astype(F32)).astype(BF16)
        red2(ch).start()

    def stage3(ch):
        red2(ch).wait_recv()
        s2[ch] = (s1[ch, y].astype(F32) + r2[ch].astype(F32)).astype(BF16)
        red3(ch).start()

    def stage4(ch):
        red3(ch).wait_recv()
        s3[ch] = (s2[ch, x].astype(F32) + r3[ch].astype(F32)).astype(BF16)
        for k in range(1, zs):
            red4(ch, k).start()

    def stage5(ch):
        total = s3[ch, z].astype(F32)
        for k in range(1, zs):
            red4(ch, k).wait_recv()
            total = total + r4[ch, k - 1].astype(F32)
        full[ch, p] = total.astype(BF16)
        for k in range(1, 4):
            red5(ch, k).start()

    def stage6(ch):
        for k in range(1, 4):
            red5(ch, k).wait_recv()
        value = full[ch].astype(F32).reshape(shard, 4 * PAIR)
        for i in range(3):
            qg_ref[:, pair_cols(ch, i * channels)] = value[:, i * PAIR : (i + 1) * PAIR]
        pg_ref[:, pair_cols(ch)] = value[:, 3 * PAIR :]

    stages = [stage1, stage2, stage3, stage4]

    def tick(t):
        pl.when(t < pairs)(lambda: backward(t))
        pl.when(jnp.logical_and(t >= 1, t <= pairs))(lambda: add_hfeat(t - 1))
        pl.when(t == pairs)(go_back)
        for i, stage in enumerate(stages):
            pl.when(jnp.logical_and(t >= i + 1, t < i + 1 + pairs))(lambda stage=stage, i=i: stage(t - i - 1))

    loop(0, pairs + len(stages), tick)
    loop(0, pairs, stage5)
    loop(1, peers, lambda k: back_copy(k).wait_recv())
    gf_ref[...] = contract_rows(place(srow), ret_buf[...].reshape(slot_rows, channels)).astype(BF16)
    outs = [pltpu.make_async_copy(src, dst, out_sem.at[i])
            for i, (src, dst) in enumerate([(gf_ref, gf_hbm), (qg_ref, qg_hbm), (pg_ref, pg_hbm)])]
    outs[0].start()
    loop(0, pairs, stage6)
    outs[1].start()
    outs[2].start()

    def sent_rows(k):
        slot_copy(k).wait_send()
        back_copy(k).wait_send()
        by_y(k).wait_send()
        by_c(k).wait_send()
        by_yc(k).wait_send()

    def sent_chunk(ch):
        dk_copy(ch).wait_send()
        for one in (red1, red2, red3):
            one(ch).wait_send()
        for k in range(1, zs):
            red4(ch, k).wait_send()
        for k in range(1, 4):
            red5(ch, k).wait_send()

    loop(1, zs, lambda k: by_z(k).wait_send())
    loop(0, zs, lambda k: by_x(k).wait_send())
    feats_copy.wait_send()
    loop(1, peers, sent_rows)
    loop(0, pairs, sent_chunk)
    for copy in outs:
        copy.wait()


def hand_over(*refs):
    count = (len(refs) - 2) // 3
    ins, outs, held = refs[:count], refs[count : 2 * count], refs[2 * count : 3 * count]
    first = [pltpu.make_async_copy(ins[i], held[i], refs[-2].at[i]) for i in range(count)]
    second = [pltpu.make_async_copy(held[i], outs[i], refs[-1].at[i]) for i in range(count)]
    for copy in first:
        copy.start()
    for i in range(count):
        first[i].wait()
        second[i].start()
    for copy in second:
        copy.wait()


def per_device(feats, grad_out, qkv_weight, proj_weight, to_hilbert, to_zorder):
    peers = lax.axis_size("rows")
    feature = feats[0]
    rows, channels = feature.shape
    blocks = to_hilbert.shape[1]
    block = rows // blocks
    slot_rows = peers * CAP * block
    zs = peers // 2
    pairs = channels // PAIR
    share, wide = qkv_weight.shape
    dma = pltpu.SemaphoreType.DMA

    def vm(*shape, kind=BF16):
        return pltpu.VMEM(shape, kind)

    width = 4 * PAIR
    scratch = [
        vm(rows, channels), vm(share, wide, kind=F32), vm(share, channels, kind=F32), dma((3,)),
        vm(peers, 4, STRIP, wide + channels),
        dma((zs - 1,)), dma((zs - 1,)), dma((zs,)), dma((zs,)),
        dma((peers - 1,)), dma((peers - 1,)), dma((2 * peers - 2,)), dma((2 * peers - 2,)),
        vm(peers, slot_rows // peers, channels), vm(peers, slot_rows // peers, channels),
        dma((peers - 1,)), dma((peers - 1,)),
        vm(peers, slot_rows // peers, channels), vm(peers, slot_rows // peers, channels),
        dma((peers - 1,)), dma((peers - 1,)),
        vm(2, rows, channels), vm(channels, 2 * rows), dma, dma,
        vm(rows, channels), vm(2 * rows, channels), vm(2 * rows, channels), vm(rows, channels),
        vm(channels, rows), vm(rows, channels), vm(rows, channels, kind=F32), vm(rows, channels, kind=F32),
        vm(2 * rows, channels), vm(2 * rows, channels), vm(rows, channels, kind=F32),
        vm(pairs, 2, rows, PAIR), vm(pairs, 2, rows, PAIR), dma((pairs,)), dma((pairs,)),
        dma((pairs, zs + 5)), dma((pairs, zs + 5)),
        vm(rows, channels), pltpu.SMEM((1, blocks), jnp.int32), pltpu.SMEM((1, blocks), jnp.int32), dma((6,)),
        vm(HEADS, 2 * rows, rows, kind=F32),
        vm(pairs, 2, 2, 2, zs, STRIP, width), vm(pairs, 2, 2, zs, STRIP, width), vm(pairs, 2, 2, zs, STRIP, width),
        vm(pairs, 2, zs, STRIP, width), vm(pairs, 2, zs, STRIP, width),
        vm(pairs, zs, STRIP, width), vm(pairs, zs, STRIP, width),
        vm(pairs, zs - 1, STRIP, width), vm(pairs, 4, STRIP, width),
    ]

    def body(*refs):
        fused_kernel(peers, slot_rows, *refs)

    shapes = (
        jax.ShapeDtypeStruct((rows, channels), BF16),
        jax.ShapeDtypeStruct((share, wide), F32),
        jax.ShapeDtypeStruct((share, channels), F32),
    )
    hbm = pl.BlockSpec(memory_space=pltpu.HBM)
    results = pl.pallas_call(
        body,
        out_shape=shapes,
        in_specs=[hbm] * 6,
        out_specs=(hbm,) * 3,
        scratch_shapes=scratch,
        compiler_params=pltpu.CompilerParams(
            collective_id=0, has_side_effects=True, vmem_limit_bytes=64 * 1024 * 1024
        ),
    )(feature, grad_out[0], qkv_weight.reshape(4, STRIP, -1), proj_weight.reshape(4, STRIP, -1), to_hilbert, to_zorder)
    grad_z, qkv_grad, proj_grad = pl.pallas_call(
        hand_over,
        out_shape=shapes,
        in_specs=[hbm] * 3,
        out_specs=(hbm,) * 3,
        scratch_shapes=[pltpu.VMEM(one.shape, one.dtype) for one in shapes] + [dma((3,)), dma((3,))],
        compiler_params=pltpu.CompilerParams(vmem_limit_bytes=64 * 1024 * 1024),
    )(*results)
    return grad_z[None], qkv_grad, proj_grad


def fits_kernel(mesh):
    return mesh.shape["rows"] == 8 and mesh.shape["rep"] == 4


def solution(mesh):
    placed = (
        P("rep", "rows", None),
        P("rep", "rows", None),
        P("rows", None),
        P("rows", None),
        P("rep", "rows"),
        P("rep", "rows"),
    )
    return jax.shard_map(
        per_device if fits_kernel(mesh) else per_device_general,
        mesh=mesh,
        in_specs=placed,
        out_specs=(P("rep", "rows", None), P("rows", None), P("rows", None)),
        check_vma=False,
    )
```

```python
import jax
import jax.numpy as jnp
from jax import lax
from jax.experimental import pallas as pl
from jax.experimental.pallas import tpu as pltpu
from jax.sharding import PartitionSpec as P

HEADS = 8
CAP = 2


def from_partner(block, axis, apart):
    count = lax.axis_size(axis)
    route = []
    for low in range(count):
        high = low | 1 << apart
        if high != low and high < count:
            route += [(low, high), (high, low)]
    return lax.ppermute(block, axis, route)


def move_blocks(outgoing):
    return lax.all_to_all(outgoing, "rows", split_axis=0, concat_axis=0, tiled=True)


def rank_within(order_keys, owners):
    same_owner = owners[None, :] == owners[:, None]
    earlier = order_keys[None, :] < order_keys[:, None]
    return jnp.sum(jnp.logical_and(same_owner, earlier).astype(jnp.int32), axis=1)


def contract_rows(left, right):
    return lax.dot_general(
        left, right, (((0,), (0,)), ((), ())), preferred_element_type=jnp.float32
    )


def contract_cols(left, right):
    return lax.dot_general(
        left, right, (((1,), (1,)), ((), ())), preferred_element_type=jnp.float32
    )


def per_device_general(feats, grad_out, qkv_weight, proj_weight, to_hilbert, to_zorder):
    peer_count = lax.axis_size("rows")
    feature = feats[0]
    rows_dev, channels = feature.shape
    head_size = channels // HEADS
    scale = head_size ** (-0.5)
    blocks_dev = to_hilbert.shape[1]
    slot_count = peer_count * CAP
    w_qkv, w_proj = (
        lax.all_gather(qkv_weight, "rows", axis=0, tiled=True),
        lax.all_gather(proj_weight, "rows", axis=0, tiled=True),
    )
    forward_list = to_hilbert[0]
    inverse_list = to_zorder[0]
    local_ids = jnp.arange(blocks_dev, dtype=jnp.int32)
    slot_ids = jnp.arange(slot_count, dtype=jnp.int32)
    target_dev = forward_list // blocks_dev
    send_slot = target_dev * CAP + rank_within(local_ids, target_dev)
    send_table = (send_slot[None, :] == slot_ids[:, None]).astype(jnp.bfloat16)
    source_dev = inverse_list // blocks_dev
    recv_slot = source_dev * CAP + rank_within(inverse_list, source_dev)
    recv_table = (recv_slot[:, None] == slot_ids[None, :]).astype(jnp.bfloat16)
    zblocks = grad_out[0].reshape(blocks_dev, -1)
    outgoing = jnp.dot(send_table, zblocks, preferred_element_type=jnp.float32).astype(jnp.bfloat16)
    arrived = move_blocks(outgoing.reshape(peer_count, CAP, -1)).reshape(slot_count, -1)
    grad_hil = jnp.dot(recv_table, arrived, preferred_element_type=jnp.float32).astype(jnp.bfloat16)
    grad_hil = grad_hil.reshape(rows_dev, channels)
    qkv = jnp.dot(feature, w_qkv, preferred_element_type=jnp.float32).astype(jnp.bfloat16)
    query = qkv[:, :channels]
    keyval = qkv[:, channels:]
    grad_attn = contract_cols(grad_hil, w_proj).astype(jnp.bfloat16)
    other_kv = from_partner(keyval, "rows", 0)
    keys_all = jnp.concatenate([keyval[:, :channels], other_kv[:, :channels]], axis=0)
    values_all = jnp.concatenate([keyval[:, channels:], other_kv[:, channels:]], axis=0)
    attn_parts, dq_parts, dk_parts, dv_parts = ([], [], [], [])
    for head_index in range(HEADS):
        lo_col = head_index * head_size
        q_head = query[:, lo_col : lo_col + head_size]
        k_head = keys_all[:, lo_col : lo_col + head_size]
        v_head = values_all[:, lo_col : lo_col + head_size]
        g_head = grad_attn[:, lo_col : lo_col + head_size]
        score = contract_cols(q_head, k_head) * scale
        row_max = jnp.max(score, axis=1, keepdims=True)
        raised = jnp.exp(score - row_max)
        row_sum = jnp.sum(raised, axis=1, keepdims=True)
        probs = raised / row_sum
        probs_b = probs.astype(jnp.bfloat16)
        attn_parts.append(
            jnp.dot(probs_b, v_head, preferred_element_type=jnp.float32).astype(jnp.bfloat16)
        )
        dprob = contract_cols(g_head, v_head)
        delta = jnp.sum(probs * dprob, axis=1, keepdims=True)
        dscore = (probs * (dprob - delta) * scale).astype(jnp.bfloat16)
        dq_parts.append(jnp.dot(dscore, k_head, preferred_element_type=jnp.float32))
        dk_parts.append(contract_rows(dscore, q_head))
        dv_parts.append(contract_rows(probs_b, g_head))
    grad_q = jnp.concatenate(dq_parts, axis=1)
    grad_k = jnp.concatenate(dk_parts, axis=1)
    grad_v = jnp.concatenate(dv_parts, axis=1)
    other_k, other_v = (
        from_partner(grad_k[rows_dev:].astype(jnp.bfloat16), "rows", 0).astype(jnp.float32),
        from_partner(grad_v[rows_dev:].astype(jnp.bfloat16), "rows", 0).astype(jnp.float32),
    )
    grad_k = grad_k[:rows_dev] + other_k
    grad_v = grad_v[:rows_dev] + other_v
    grad_qkv = jnp.concatenate([grad_q, grad_k, grad_v], axis=1).astype(jnp.bfloat16)
    attn = jnp.concatenate(attn_parts, axis=1)
    grad_hfeat = contract_cols(grad_qkv, w_qkv).astype(jnp.bfloat16)
    hblocks = grad_hfeat.reshape(blocks_dev, -1)
    going_back = contract_rows(recv_table, hblocks).astype(jnp.bfloat16)
    returned = move_blocks(going_back.reshape(peer_count, CAP, -1)).reshape(slot_count, -1)
    grad_z = contract_rows(send_table, returned).astype(jnp.bfloat16).reshape(rows_dev, channels)
    share = channels // peer_count
    term = jnp.concatenate(
        [contract_rows(feature, grad_qkv), contract_rows(attn, grad_hil)], axis=1
    )
    total = lax.psum(term, ("rows", "rep"))
    owned = lax.dynamic_slice_in_dim(total, lax.axis_index("rows") * share, share, 0)
    return (grad_z[None], owned[:, : 3 * channels], owned[:, 3 * channels :])


MESH = pl.DeviceIdType.MESH
PAIR = 128
STRIP = 16
F32 = jnp.float32
BF16 = jnp.bfloat16


def dot(left, right):
    return jnp.dot(left, right, preferred_element_type=F32)


def slot_of_row(owners, order_keys, block, rows):
    lane = lax.broadcasted_iota(jnp.int32, (1, rows), 1)
    out = lax.rem(lane, block)
    for i, owner in enumerate(owners):
        rank = jnp.int32(0)
        for j, other in enumerate(owners):
            if j != i:
                rank += jnp.where(jnp.logical_and(other == owner, order_keys[j] < order_keys[i]), 1, 0)
        out += jnp.where(lax.div(lane, block) == i, (owner * CAP + rank) * block, 0)
    return out


def fused_kernel(peers, slot_rows, feats_hbm, grad_hbm, wq_hbm, wp_hbm, toh_hbm, toz_hbm,
                 gf_hbm, qg_hbm, pg_hbm,
                 gf_ref, qg_ref, pg_ref, out_sem, wf, wz_s, wz_r, wx_s, wx_r, wy_s, wy_r, wc_s, wc_r,
                 out_buf, arr_buf, sl_s, sl_r, back_buf, ret_buf, bk_s, bk_r,
                 fa, ft, ff_s, ff_r, q_v, k_v, v_v, h_v, at_v, dq_v, dk_v, dv_v, dkb_v, dvb_v, hf_v,
                 dks, dkr, dk_s, dk_r, red_s, red_r, grad_v, toh, toz, in_sem, probs_v,
                 term, r1, s1, r2, s2, r3, s3, r4, full):
    rows, channels = feats_hbm.shape
    blocks = toh_hbm.shape[1]
    wide = wq_hbm.shape[2]
    pairs = channels // PAIR
    shard = 4 * STRIP
    half = channels // 2
    r = lax.axis_index("rows")
    p = lax.axis_index("rep")
    x, z = lax.rem(r, 2), lax.div(r, 2)
    c, y = lax.rem(p, 2), lax.div(p, 2)
    across_x = (r + 1 - 2 * x, p)
    across_c = (r, p + 1 - 2 * c)
    across_y = (r, p + 2 - 4 * y)
    zs = peers // 2

    def remote(src, dst, send_sem, recv_sem, device):
        return pltpu.make_async_remote_copy(
            src_ref=src, dst_ref=dst, send_sem=send_sem, recv_sem=recv_sem,
            device_id=device, device_id_type=MESH)

    def loop(lo, hi, body):
        lax.fori_loop(lo, hi, lambda i, carry: (body(i), carry)[1], 0)

    loads = []
    for i, (src, dst) in enumerate([(toh_hbm, toh), (toz_hbm, toz), (grad_hbm, grad_v),
                                    (wp_hbm, wf.at[1, r, :, :, pl.ds(wide // 2, channels)]),
                                    (feats_hbm, fa.at[0])]
                                   + [(wq_hbm.at[:, :, pl.ds(j * channels + w * half, half)],
                                       wf.at[w, r, :, :, pl.ds(j * half, half)])
                                      for w in range(2) for j in range(3)]):
        copy = pltpu.make_async_copy(src, dst, in_sem.at[i])
        copy.start()
        loads.append(copy)

    barrier = pltpu.get_barrier_semaphore()

    def greet(device):
        pl.semaphore_signal(barrier, inc=1, device_id=device, device_id_type=MESH)

    loop(1, peers, lambda k: greet((lax.rem(r + k, peers), p)))
    loop(1, 4, lambda k: greet((r, lax.rem(p + k, 4))))


    def place(row):
        return jnp.where(slot_ids == row, 1.0, 0.0).astype(BF16)

    per_peer = slot_rows // peers
    for copy in [loads[3]] + loads[5:]:
        copy.wait()
    pl.semaphore_wait(barrier, peers - 1 + 3)

    def row_of(j):
        return lax.rem(z + zs - lax.rem(j, zs), zs) * 2 + lax.rem(x + lax.div(j, zs), 2)

    class Wave:
        def __init__(self, w):
            self.w, self.cols = w, pl.ds(0, wide // 2 if w == 0 else wide // 2 + channels)

        def strip_copy(self, row, strip, s_sem, r_sem, i, device):
            ref = wf.at[self.w, row, strip, :, self.cols]
            return remote(ref, ref, s_sem.at[self.w, i], r_sem.at[self.w, i], device)

        def by_z(self, k):
            return self.strip_copy(r, p, wz_s, wz_r, k - 1, (lax.rem(z + k, zs) * 2 + x, p))

        def by_x(self, k):
            return self.strip_copy(row_of(k), p, wx_s, wx_r, k, across_x)

        def by_y(self, j):
            return self.strip_copy(row_of(j), p, wy_s, wy_r, j - 1, across_y)

        def by_c(self, j):
            return self.strip_copy(row_of(j), p, wc_s, wc_r, j - 1, across_c)

        def by_yc(self, j):
            return self.strip_copy(row_of(j), p + 2 - 4 * y, wc_s, wc_r, peers - 2 + j, across_c)

        def start(self):
            loop(1, zs, lambda k: self.by_z(k).start())
            self.by_x(0).start()

        def after_z(self):
            def one(k):
                self.by_z(k).wait_recv()
                self.by_x(k).start()
                self.by_y(k).start()
                self.by_c(k).start()
            loop(1, zs, one)

        def after_x(self):
            def one(k):
                self.by_x(k).wait_recv()
                self.by_y(zs + k).start()
                self.by_c(zs + k).start()
            loop(0, zs, one)

        def after_y(self):
            def one(j):
                self.by_y(j).wait_recv()
                self.by_yc(j).start()
            loop(1, peers, one)

        def after_c(self):
            def one(j):
                self.by_c(j).wait_recv()
                self.by_yc(j).wait_recv()
            loop(1, peers, one)

        def sent(self):
            def one(j):
                self.by_y(j).wait_send()
                self.by_c(j).wait_send()
                self.by_yc(j).wait_send()
            loop(1, zs, lambda k: self.by_z(k).wait_send())
            loop(0, zs, lambda k: self.by_x(k).wait_send())
            loop(1, peers, one)

    near, far = Wave(0), Wave(1)

    def slot_copy(k):
        d = lax.rem(r + k, peers)
        return remote(out_buf.at[d], arr_buf.at[r], sl_s.at[k - 1], sl_r.at[k - 1], (d, p))

    def back_copy(k):
        d = lax.rem(r + k, peers)
        return remote(back_buf.at[d], ret_buf.at[r], bk_s.at[k - 1], bk_r.at[k - 1], (d, p))

    feats_copy = remote(fa.at[0], fa.at[1], ff_s, ff_r, across_x)

    near.start()
    for copy in loads[:2]:
        copy.wait()
    forward_list = [toh[0, i] for i in range(blocks)]
    inverse_list = [toz[0, i] for i in range(blocks)]
    srow = slot_of_row([lax.div(b, blocks) for b in forward_list], list(range(blocks)), rows // blocks, rows)
    rrow = slot_of_row([lax.div(b, blocks) for b in inverse_list], inverse_list, rows // blocks, rows)
    slot_ids = lax.broadcasted_iota(jnp.int32, (slot_rows, rows), 0)
    loads[2].wait()
    out_buf[...] = dot(place(srow), grad_v[...]).astype(BF16).reshape(peers, per_peer, channels)
    arr_buf[r] = out_buf[r]

    near.after_z()
    far.start()
    loads[4].wait()
    feats_copy.start()
    near.after_x()
    far.after_z()
    loop(1, peers, lambda k: slot_copy(k).start())
    feats_copy.wait_recv()

    def turn(i):
        ft[:, pl.ds(pl.multiple_of(i * rows, rows), rows)] = fa[i].astype(F32).T.astype(BF16)

    loop(0, 2, turn)
    near.after_y()
    far.after_x()
    near.after_c()

    def pair_cols(hp, base=0):
        return pl.ds(pl.multiple_of(base + hp * PAIR, PAIR), PAIR)

    def weight(i, hp):
        return wf[lax.div(hp, 2), :, :, :, pair_cols(lax.rem(hp, 2), i * half)].reshape(shard * peers, PAIR)

    head_size = channels // HEADS
    scale = head_size ** (-0.5)
    log2e = 1.4426950408889634
    lane = lax.broadcasted_iota(jnp.int32, (1, PAIR), 1)
    masks = [jnp.where(lane < head_size, 1.0, 0.0).astype(BF16), jnp.where(lane < head_size, 0.0, 1.0).astype(BF16)]

    def forward(hp):
        cols = pair_cols(hp)
        both = fa[...].reshape(2 * rows, channels)
        qp = dot(fa[0], weight(0, hp)).astype(BF16)
        kp = dot(both, weight(1, hp)).astype(BF16)
        vp = dot(both, weight(2, hp)).astype(BF16)
        q_v[:, cols], k_v[:, cols], v_v[:, cols] = qp, kp, vp
        v_t = vp.astype(F32).T.astype(BF16)
        parts = []
        for e in range(2):
            score = contract_cols(kp, qp * masks[e])
            raised = jnp.exp2((score - jnp.max(score, axis=0, keepdims=True)) * (scale * log2e))
            probs = raised * (1.0 / jnp.sum(raised, axis=0, keepdims=True))
            probs_v[2 * hp + e] = probs
            parts.append(dot(v_t[e * head_size : (e + 1) * head_size], probs.astype(BF16)))
        at_v[cols, :] = jnp.concatenate(parts, axis=0).astype(BF16)

    loop(0, pairs // 2, forward)
    far.after_y()
    far.after_c()
    loop(pairs // 2, pairs, forward)
    loop(1, peers, lambda k: slot_copy(k).wait_recv())
    h_v[...] = contract_rows(place(rrow), arr_buf[...].reshape(slot_rows, channels)).astype(BF16)
    hf_v[...] = jnp.zeros_like(hf_v)

    def dk_copy(hp):
        return remote(dks.at[hp], dkr.at[hp], dk_s.at[hp], dk_r.at[hp], across_x)

    def backward(hp):
        cols = pair_cols(hp)
        qp, kp, vp = q_v[:, cols], k_v[:, cols], v_v[:, cols]
        w_rows = wf[1, pl.ds(hp * (PAIR // shard), PAIR // shard), :, :, wide // 2 :].reshape(PAIR, channels)
        gp = contract_cols(h_v[...], w_rows).astype(BF16)
        k_t = kp.astype(F32).T.astype(BF16)
        dk = dv = None
        dq_t = []
        for e in range(2):
            mine = slice(e * head_size, (e + 1) * head_size)
            qm, gm = qp * masks[e], gp * masks[e]
            probs = probs_v[2 * hp + e]
            probs_b = probs.astype(BF16)
            dprob = contract_cols(vp, gm)
            delta = jnp.sum(probs * dprob, axis=0, keepdims=True)
            dscore = (probs * (dprob - delta)).astype(BF16)
            dq_t.append(dot(k_t[mine], dscore))
            dk_e, dv_e = dot(dscore, qm), dot(probs_b, gm)
            dk = dk_e if dk is None else dk + dk_e
            dv = dv_e if dv is None else dv + dv_e
        dk = dk * scale
        dk_b, dv_b = dk.astype(BF16), dv.astype(BF16)
        dks[hp, 0] = dk_b[rows:]
        dks[hp, 1] = dv_b[rows:]
        dk_copy(hp).start()
        dq_v[:, cols] = (jnp.concatenate(dq_t, axis=0) * scale).T.astype(BF16)
        dk_v[:, cols], dv_v[:, cols] = dk[:rows], dv[:rows]
        dkb_v[:, cols], dvb_v[:, cols] = dk_b, dv_b

    def add_hfeat(hp):
        cols = pair_cols(hp)
        dk_copy(hp).wait_recv()
        dk = (dk_v[:, cols] + dkr[hp, 0].astype(F32)).astype(BF16)
        dv = (dv_v[:, cols] + dkr[hp, 1].astype(F32)).astype(BF16)
        left = jnp.concatenate([dq_v[:, cols], dk, dv], axis=1)
        right = jnp.concatenate([weight(i, hp) for i in range(3)], axis=1)
        hf_v[...] += contract_cols(left, right)

    def go_back():
        back_buf[...] = dot(place(rrow), hf_v[...].astype(BF16)).astype(BF16).reshape(peers, per_peer, channels)
        ret_buf[r] = back_buf[r]
        loop(1, peers, lambda k: back_copy(k).start())

    def red(ch, i, src, dst, device):
        return remote(src, dst, red_s.at[ch, i], red_r.at[ch, i], device)

    def red1(ch):
        return red(ch, 0, term.at[ch, 1 - c], r1.at[ch], across_c)

    def red2(ch):
        return red(ch, 1, s1.at[ch, 1 - y], r2.at[ch], across_y)

    def red3(ch):
        return red(ch, 2, s2.at[ch, 1 - x], r3.at[ch], across_x)

    def red4(ch, k):
        zz = lax.rem(z + k, zs)
        return red(ch, 2 + k, s3.at[ch, zz], r4.at[ch, k - 1], (zz * 2 + x, p))

    def red5(ch, k):
        return red(ch, 1 + zs + k, full.at[ch, p], full.at[ch, p], (r, lax.rem(p + k, 4)))

    def stage1(ch):
        cols = pair_cols(ch)
        parts = [dot(ft[:, 0:rows], dq_v[:, cols]), dot(ft[...], dkb_v[:, cols]), dot(ft[...], dvb_v[:, cols]),
                 dot(at_v[...], h_v[:, cols])]
        for j, part in enumerate(parts):
            part = part.astype(BF16)
            for i in range(4 * peers):
                cc, yy, xx, zz = i % 2, i // 2 % 2, i // 4 % 2, i // 8
                term[ch, cc, yy, xx, zz, :, j * PAIR : (j + 1) * PAIR] = part[i * STRIP : (i + 1) * STRIP, :]
        red1(ch).start()

    def stage2(ch):
        red1(ch).wait_recv()
        s1[ch] = (term[ch, c].astype(F32) + r1[ch].astype(F32)).astype(BF16)
        red2(ch).start()

    def stage3(ch):
        red2(ch).wait_recv()
        s2[ch] = (s1[ch, y].astype(F32) + r2[ch].astype(F32)).astype(BF16)
        red3(ch).start()

    def stage4(ch):
        red3(ch).wait_recv()
        s3[ch] = (s2[ch, x].astype(F32) + r3[ch].astype(F32)).astype(BF16)
        for k in range(1, zs):
            red4(ch, k).start()

    def stage5(ch):
        total = s3[ch, z].astype(F32)
        for k in range(1, zs):
            red4(ch, k).wait_recv()
            total = total + r4[ch, k - 1].astype(F32)
        full[ch, p] = total.astype(BF16)
        for k in range(1, 4):
            red5(ch, k).start()

    def stage6(ch):
        for k in range(1, 4):
            red5(ch, k).wait_recv()
        value = full[ch].astype(F32).reshape(shard, 4 * PAIR)
        for i in range(3):
            qg_ref[:, pair_cols(ch, i * channels)] = value[:, i * PAIR : (i + 1) * PAIR]
        pg_ref[:, pair_cols(ch)] = value[:, 3 * PAIR :]

    stages = [stage1, stage2, stage3, stage4]

    def tick(t):
        pl.when(t < pairs)(lambda: backward(t))
        pl.when(jnp.logical_and(t >= 1, t <= pairs))(lambda: add_hfeat(t - 1))
        pl.when(t == pairs)(go_back)
        for i, stage in enumerate(stages):
            pl.when(jnp.logical_and(t >= i + 1, t < i + 1 + pairs))(lambda stage=stage, i=i: stage(t - i - 1))

    loop(0, pairs + len(stages), tick)
    loop(0, pairs, stage5)
    loop(1, peers, lambda k: back_copy(k).wait_recv())
    gf_ref[...] = contract_rows(place(srow), ret_buf[...].reshape(slot_rows, channels)).astype(BF16)
    outs = [pltpu.make_async_copy(src, dst, out_sem.at[i])
            for i, (src, dst) in enumerate([(gf_ref, gf_hbm), (qg_ref, qg_hbm), (pg_ref, pg_hbm)])]
    outs[0].start()
    loop(0, pairs, stage6)
    outs[1].start()
    outs[2].start()

    def sent_rows(k):
        slot_copy(k).wait_send()
        back_copy(k).wait_send()

    def sent_chunk(ch):
        dk_copy(ch).wait_send()
        for one in (red1, red2, red3):
            one(ch).wait_send()
        for k in range(1, zs):
            red4(ch, k).wait_send()
        for k in range(1, 4):
            red5(ch, k).wait_send()

    near.sent()
    far.sent()
    feats_copy.wait_send()
    loop(1, peers, sent_rows)
    loop(0, pairs, sent_chunk)
    for copy in outs:
        copy.wait()


def hand_over(*refs):
    count = (len(refs) - 2) // 3
    ins, outs, held = refs[:count], refs[count : 2 * count], refs[2 * count : 3 * count]
    first = [pltpu.make_async_copy(ins[i], held[i], refs[-2].at[i]) for i in range(count)]
    second = [pltpu.make_async_copy(held[i], outs[i], refs[-1].at[i]) for i in range(count)]
    for copy in first:
        copy.start()
    for i in range(count):
        first[i].wait()
        second[i].start()
    for copy in second:
        copy.wait()


def per_device(feats, grad_out, qkv_weight, proj_weight, to_hilbert, to_zorder):
    peers = lax.axis_size("rows")
    feature = feats[0]
    rows, channels = feature.shape
    blocks = to_hilbert.shape[1]
    block = rows // blocks
    slot_rows = peers * CAP * block
    zs = peers // 2
    pairs = channels // PAIR
    share, wide = qkv_weight.shape
    dma = pltpu.SemaphoreType.DMA

    def vm(*shape, kind=BF16):
        return pltpu.VMEM(shape, kind)

    width = 4 * PAIR
    scratch = [
        vm(rows, channels), vm(share, wide, kind=F32), vm(share, channels, kind=F32), dma((3,)),
        vm(2, peers, 4, STRIP, wide // 2 + channels),
        dma((2, zs - 1)), dma((2, zs - 1)), dma((2, zs)), dma((2, zs)),
        dma((2, peers - 1)), dma((2, peers - 1)), dma((2, 2 * peers - 2)), dma((2, 2 * peers - 2)),
        vm(peers, slot_rows // peers, channels), vm(peers, slot_rows // peers, channels),
        dma((peers - 1,)), dma((peers - 1,)),
        vm(peers, slot_rows // peers, channels), vm(peers, slot_rows // peers, channels),
        dma((peers - 1,)), dma((peers - 1,)),
        vm(2, rows, channels), vm(channels, 2 * rows), dma, dma,
        vm(rows, channels), vm(2 * rows, channels), vm(2 * rows, channels), vm(rows, channels),
        vm(channels, rows), vm(rows, channels), vm(rows, channels, kind=F32), vm(rows, channels, kind=F32),
        vm(2 * rows, channels), vm(2 * rows, channels), vm(rows, channels, kind=F32),
        vm(pairs, 2, rows, PAIR), vm(pairs, 2, rows, PAIR), dma((pairs,)), dma((pairs,)),
        dma((pairs, zs + 5)), dma((pairs, zs + 5)),
        vm(rows, channels), pltpu.SMEM((1, blocks), jnp.int32), pltpu.SMEM((1, blocks), jnp.int32), dma((11,)),
        vm(HEADS, 2 * rows, rows, kind=F32),
        vm(pairs, 2, 2, 2, zs, STRIP, width), vm(pairs, 2, 2, zs, STRIP, width), vm(pairs, 2, 2, zs, STRIP, width),
        vm(pairs, 2, zs, STRIP, width), vm(pairs, 2, zs, STRIP, width),
        vm(pairs, zs, STRIP, width), vm(pairs, zs, STRIP, width),
        vm(pairs, zs - 1, STRIP, width), vm(pairs, 4, STRIP, width),
    ]

    def body(*refs):
        fused_kernel(peers, slot_rows, *refs)

    shapes = (
        jax.ShapeDtypeStruct((rows, channels), BF16),
        jax.ShapeDtypeStruct((share, wide), F32),
        jax.ShapeDtypeStruct((share, channels), F32),
    )
    hbm = pl.BlockSpec(memory_space=pltpu.HBM)
    results = pl.pallas_call(
        body,
        out_shape=shapes,
        in_specs=[hbm] * 6,
        out_specs=(hbm,) * 3,
        scratch_shapes=scratch,
        compiler_params=pltpu.CompilerParams(
            collective_id=0, has_side_effects=True, vmem_limit_bytes=64 * 1024 * 1024
        ),
    )(feature, grad_out[0], qkv_weight.reshape(4, STRIP, -1), proj_weight.reshape(4, STRIP, -1), to_hilbert, to_zorder)
    grad_z, qkv_grad, proj_grad = pl.pallas_call(
        hand_over,
        out_shape=shapes,
        in_specs=[hbm] * 3,
        out_specs=(hbm,) * 3,
        scratch_shapes=[pltpu.VMEM(one.shape, one.dtype) for one in shapes] + [dma((3,)), dma((3,))],
        compiler_params=pltpu.CompilerParams(vmem_limit_bytes=64 * 1024 * 1024),
    )(*results)
    return grad_z[None], qkv_grad, proj_grad


def fits_kernel(mesh):
    return mesh.shape["rows"] == 8 and mesh.shape["rep"] == 4


def solution(mesh):
    placed = (
        P("rep", "rows", None),
        P("rep", "rows", None),
        P("rows", None),
        P("rows", None),
        P("rep", "rows"),
        P("rep", "rows"),
    )
    return jax.shard_map(
        per_device if fits_kernel(mesh) else per_device_general,
        mesh=mesh,
        in_specs=placed,
        out_specs=(P("rep", "rows", None), P("rows", None), P("rows", None)),
        check_vma=False,
    )
```
